32 devices in a mesh: groups: 2 (over y), lon: 4 (over x, core), lat: 4 (over z).
Axes of the slice: x: 2, y: 2, z: 4, core: 2. Of those that a mesh axis runs over, the one named last changes fastest.
Arguments:
- heat_anomaly: float32 [16, 1024, 512], P('groups', 'lat', 'lon'), parts along dimension 0, may hold values from -6 to 6
- zonal_speed: float32 [16, 1024, 512], P('groups', 'lat', 'lon'), parts along dimension 0, may hold values from -18 to 18
- meridional_speed: float32 [16, 1024, 512], P('groups', 'lat', 'lon'), parts along dimension 0, may hold values from -18 to 18
- submerged_tiers_per_site: int32 [2048, 512], P(('groups', 'lat'), 'lon'), parts along dimension 0, may hold values from 0 to 8, as said below
Outputs:
- heat_anomaly_next: float32 [16, 1024, 512], P('groups', 'lat', 'lon'), parts along dimension 0
- zonal_speed_next: float32 [16, 1024, 512], P('groups', 'lat', 'lon'), parts along dimension 0
- meridional_speed_next: float32 [16, 1024, 512], P('groups', 'lat', 'lon'), parts along dimension 0
- free_height_anomaly: float32 [2048, 512], P(('groups', 'lat'), 'lon'), parts along dimension 0
The draws below stay inside these ranges and needn't reach their ends.
There are 2 independent parts, one for each index of `groups`. The reference program is written for one: setup_inputs(seed, part) draws one part's arguments, and reference() takes and returns one part's arrays. A program takes and returns all parts, laid end to end along the dimension named above; each array names one. Nothing has to cross between parts.
Inputs may be any that keep to these rules, and one draw needn't show every extreme that they name: `submerged_tiers_per_site`: blocks of 8 x 128 cells tile the grid from row 0 and column 0; every cell of a land block is 0, the first cell of an ocean block is 1 or more; each band of 256 rows that starts at a multiple of 256 holds exactly 96 ocean blocks.
All inputs are finite; a program needn't handle non-finite values.
Results may differ from the reference program's by a relative error of at most 0.00015.
Values sent between devices are 32-bit elements; how exact they have to be, the bound alone decides.
A program may use at most 64 MiB of HBM per device.

```python
import jax
import jax.numpy as jnp
from jax import lax

VERTICAL_TIERS = 8
BY = 8
BX = 128
CY = 256
ITERS = 4
NB = 32
CAP = 24
PARALLEL_POINTS = 512
MERIDIAN_POINTS = 1024


def lon_growth():
    position = jnp.arange(PARALLEL_POINTS).astype(jnp.float32)
    return 1.0 + 2.0 * position / max(PARALLEL_POINTS - 1, 1)


def draw_zonal_speed(key, part):
    key = jax.random.fold_in(key, 11)
    normals_key = jax.random.fold_in(key, 0)
    values = jax.random.normal(normals_key, (VERTICAL_TIERS, MERIDIAN_POINTS, PARALLEL_POINTS), jnp.float32)
    return jnp.clip(values * lon_growth(), -18.0, 18.0)


def draw_meridional_speed(key, part):
    key = jax.random.fold_in(key, 12)
    normals_key = jax.random.fold_in(key, 0)
    values = jax.random.normal(normals_key, (VERTICAL_TIERS, MERIDIAN_POINTS, PARALLEL_POINTS), jnp.float32)
    return jnp.clip(values * lon_growth(), -18.0, 18.0)


def draw_submerged_tiers_per_site(key, part):
    key = jax.random.fold_in(key, 5)
    chooser, levels_key = jax.random.split(key)
    columns = PARALLEL_POINTS // BX
    bands = MERIDIAN_POINTS // CY
    orders = jax.vmap(lambda band_key: jax.random.permutation(band_key, columns * NB))(jax.random.split(chooser, bands))
    ocean_block = (orders < columns * CAP).reshape(bands, columns, NB)
    ocean_block = jnp.transpose(ocean_block, (0, 2, 1)).reshape(bands * NB, columns)
    ocean_cells = jnp.repeat(jnp.repeat(ocean_block, BY, axis=0), BX, axis=1)
    depth_drawn = jax.random.randint(levels_key, (MERIDIAN_POINTS, PARALLEL_POINTS), 0, VERTICAL_TIERS + 1)
    row_index = lax.broadcasted_iota(jnp.int32, (MERIDIAN_POINTS, PARALLEL_POINTS), 0)
    col_index = lax.broadcasted_iota(jnp.int32, (MERIDIAN_POINTS, PARALLEL_POINTS), 1)
    corner = (row_index % BY == 0) & (col_index % BX == 0)
    depth_drawn = jnp.where(corner, jnp.maximum(depth_drawn, 1), depth_drawn)
    return jnp.where(ocean_cells, depth_drawn, 0).astype(jnp.int32)


def level_of(key, shape, shards, least, high):
    factor_of = 1.0
    for axis_at, blocks in shards:
        heights = jax.random.uniform(jax.random.fold_in(jax.random.fold_in(key, 6), axis_at), (blocks,), jnp.float32, least / len(shards), high / len(shards))
        factor_of = factor_of * jnp.repeat(jnp.exp(heights), shape[axis_at] // blocks).reshape((-1,) + (1,) * (len(shape) - 1 - axis_at))
    return factor_of


def scatter_about(own_key, shape, deviation, bound, pieces=(), dtype=jnp.bfloat16):
    drawn = deviation * jax.random.normal(own_key, shape, jnp.float32)
    if pieces:
        drawn = drawn * level_of(own_key, shape, pieces, -0.22, 0.18)
    return jnp.clip(drawn, -bound, bound).astype(dtype)


def setup_inputs(seed: int = 0, part: int = 0) -> dict:
    streams_of = jax.random.split(jax.random.key(seed), 5)
    part_splits = jax.random.split(jax.random.fold_in(streams_of[4], part), 5)
    heat_anomaly = scatter_about(part_splits[0], (VERTICAL_TIERS, MERIDIAN_POINTS, PARALLEL_POINTS), 1.0, 6.0, ((1, 4), (2, 4)), jnp.float32)
    zonal_speed = draw_zonal_speed(jax.random.fold_in(jax.random.fold_in(streams_of[4], part), 71), part)
    meridional_speed = draw_meridional_speed(jax.random.fold_in(jax.random.fold_in(streams_of[4], part), 71), part)
    submerged_tiers_per_site = draw_submerged_tiers_per_site(jax.random.fold_in(jax.random.fold_in(streams_of[4], part), 71), part)
    return {"heat_anomaly": heat_anomaly, "zonal_speed": zonal_speed, "meridional_speed": meridional_speed, "submerged_tiers_per_site": submerged_tiers_per_site}


TIME_STEP = 0.05
DIFFUSIVITY = 0.2
VISCOSITY = 0.2
HEAT_DILATION = 0.5
SURFACE_TERM = 0.01
ROW_DECAY = 0.6
COLUMN_DECAY = 0.6

def layer_thickness(tier_number):
    position = jnp.arange(tier_number).astype(jnp.float32)
    return (position + 1.0) * (2.0 / (tier_number * (tier_number + 1)))

def decay_matrix(extent, decay_rate):
    position = jnp.arange(extent)
    distance = jnp.abs(position[:, None] - position[None, :]).astype(jnp.float32)
    return decay_rate ** distance

def block_kernel(blocks, across_rows, across_cols):
    inner = jnp.einsum('ij,bjk->bik', across_rows, blocks, precision=lax.Precision.HIGHEST)
    return jnp.einsum('bik,kl->bil', inner, across_cols, precision=lax.Precision.HIGHEST)

def vertical_shear_part(heat_anomaly, zonal_current, meridional_current, marine_indicator, rotation_parameter, tier_floor, basin_pieces):
    weight_load = -HEAT_DILATION * jnp.cumsum(tier_floor[:, None, None] * heat_anomaly, axis=0)
    wet_mid, wet_east, wet_west, wet_north, wet_south = basin_pieces(marine_indicator)
    face_east = wet_mid * wet_east
    face_west = wet_mid * wet_west
    face_north = wet_mid * wet_north
    face_south = wet_mid * wet_south
    scalar_middle, scalar_right, scalar_left, scalar_upper, scalar_lower = basin_pieces(heat_anomaly)
    zonal_mid, zonal_east, zonal_west, zonal_north, zonal_south = basin_pieces(zonal_current)
    meridional_mid, meridional_east, meridional_west, meridional_north, meridional_south = basin_pieces(meridional_current)
    pressure_mid, pressure_east, pressure_west, pressure_north, pressure_south = basin_pieces(weight_load)
    diffusion = DIFFUSIVITY * (face_east * (scalar_right - scalar_middle) + face_west * (scalar_left - scalar_middle) + face_north * (scalar_upper - scalar_middle) + face_south * (scalar_lower - scalar_middle))
    advection = 0.25 * (face_east * (zonal_mid + zonal_east) * (scalar_middle + scalar_right) - face_west * (zonal_mid + zonal_west) * (scalar_middle + scalar_left) + face_north * (meridional_mid + meridional_north) * (scalar_middle + scalar_upper) - face_south * (meridional_mid + meridional_south) * (scalar_middle + scalar_lower))
    tracer_next = wet_mid * (scalar_middle + TIME_STEP * (diffusion - advection))
    slope_x = 0.5 * (face_east * (pressure_east - pressure_mid) + face_west * (pressure_mid - pressure_west))
    slope_y = 0.5 * (face_north * (pressure_north - pressure_mid) + face_south * (pressure_mid - pressure_south))
    spread_zonal = face_east * (zonal_east - zonal_mid) + face_west * (zonal_west - zonal_mid) + face_north * (zonal_north - zonal_mid) + face_south * (zonal_south - zonal_mid)
    spread_meridional = face_east * (meridional_east - meridional_mid) + face_west * (meridional_west - meridional_mid) + face_north * (meridional_north - meridional_mid) + face_south * (meridional_south - meridional_mid)
    zonal_speed_next = wet_mid * (zonal_mid + TIME_STEP * (rotation_parameter * meridional_mid - slope_x + VISCOSITY * spread_zonal))
    meridional_speed_next = wet_mid * (meridional_mid + TIME_STEP * (-rotation_parameter * zonal_mid - slope_y + VISCOSITY * spread_meridional))
    return (tracer_next, zonal_speed_next, meridional_speed_next)

def barotropic_forcing(wet_mid, transport_x, transport_y):
    return -wet_mid * 0.5 * (transport_x[1] - transport_x[2] + (transport_y[3] - transport_y[4]))

def surface_coefficients(wet_pieces, depth_pieces):
    wet_mid, wet_east, wet_west, wet_north, wet_south = wet_pieces
    depth_mid, depth_east, depth_west, depth_north, depth_south = depth_pieces
    link_east = wet_mid * wet_east * 0.5 * (depth_mid + depth_east)
    link_west = wet_mid * wet_west * 0.5 * (depth_mid + depth_west)
    link_north = wet_mid * wet_north * 0.5 * (depth_mid + depth_north)
    link_south = wet_mid * wet_south * 0.5 * (depth_mid + depth_south)
    diagonal = SURFACE_TERM + link_east + link_west + link_north + link_south
    return (diagonal, (link_east, link_west, link_north, link_south))

def apply_surface(quantity, neighbours, wet_mid, diagonal, links):
    return wet_mid * (diagonal * quantity - (links[0] * neighbours[0] + links[1] * neighbours[1] + links[2] * neighbours[2] + links[3] * neighbours[3]))

def entire_basin_pieces(values):
    east = jnp.roll(values, -1, axis=-1)
    west = jnp.roll(values, 1, axis=-1)
    filler = jnp.zeros_like(values[..., :1, :])
    north = jnp.concatenate([values[..., 1:, :], filler], axis=-2)
    south = jnp.concatenate([filler, values[..., :-1, :]], axis=-2)
    return (values, east, west, north, south)

def reference(heat_anomaly, zonal_speed, meridional_speed, submerged_tiers_per_site):
    tier_floor = layer_thickness(VERTICAL_TIERS)
    marine_indicator = (jnp.arange(VERTICAL_TIERS).astype(jnp.int32)[:, None, None] < submerged_tiers_per_site[None]).astype(jnp.float32)
    latitude = jnp.arange(MERIDIAN_POINTS).astype(jnp.float32)
    rotation_parameter = (2.0 * (latitude + 0.5) / MERIDIAN_POINTS - 1.0)[:, None]
    heat_anomaly_next, zonal_speed_next, meridional_speed_next = vertical_shear_part(heat_anomaly, zonal_speed, meridional_speed, marine_indicator, rotation_parameter, tier_floor, entire_basin_pieces)
    transport_x = lax.optimization_barrier(jnp.sum(tier_floor[:, None, None] * zonal_speed_next, axis=0))
    transport_y = lax.optimization_barrier(jnp.sum(tier_floor[:, None, None] * meridional_speed_next, axis=0))
    column_depth = lax.optimization_barrier(jnp.sum(tier_floor[:, None, None] * marine_indicator, axis=0))
    wet_pieces = entire_basin_pieces(marine_indicator[0])
    wet_mid = wet_pieces[0]
    forcing = barotropic_forcing(wet_mid, entire_basin_pieces(transport_x), entire_basin_pieces(transport_y))
    diagonal, links = surface_coefficients(wet_pieces, entire_basin_pieces(column_depth))
    inverse_root = 1.0 / jnp.sqrt(diagonal)
    across_rows = decay_matrix(BY, ROW_DECAY)
    across_cols = decay_matrix(BX, COLUMN_DECAY)

    def operate(quantity):
        return apply_surface(quantity, entire_basin_pieces(quantity)[1:], wet_mid, diagonal, links)

    def condition(quantity):
        scaled = wet_mid * inverse_root * quantity
        blocks = scaled.reshape(MERIDIAN_POINTS // BY, BY, PARALLEL_POINTS // BX, BX).transpose(0, 2, 1, 3).reshape(-1, BY, BX)
        result = block_kernel(blocks, across_rows, across_cols)
        result = result.reshape(MERIDIAN_POINTS // BY, PARALLEL_POINTS // BX, BY, BX).transpose(0, 2, 1, 3).reshape(MERIDIAN_POINTS, PARALLEL_POINTS)
        return wet_mid * inverse_root * result
    free_height_anomaly = jnp.zeros((MERIDIAN_POINTS, PARALLEL_POINTS), jnp.float32)
    residual = forcing
    conditioned = condition(residual)
    direction = conditioned
    progress = jnp.sum(residual * conditioned)
    for iteration in range(ITERS):
        applied = operate(direction)
        step_size = progress / jnp.sum(direction * applied)
        free_height_anomaly = free_height_anomaly + step_size * direction
        residual = residual - step_size * applied
        if iteration + 1 < ITERS:
            conditioned = condition(residual)
            following = jnp.sum(residual * conditioned)
            direction = conditioned + following / progress * direction
            progress = following
    return (heat_anomaly_next, zonal_speed_next, meridional_speed_next, free_height_anomaly)
```

```python
import functools

import jax
import jax.numpy as jnp
import ml_dtypes
import numpy as np
from jax import lax
from jax.experimental import pallas as pl
from jax.experimental.pallas import tpu as pltpu
from jax.sharding import PartitionSpec as P

BY = 8
ITERS = 4
TIME_STEP = 0.05
DIFFUSIVITY = 0.2
VISCOSITY = 0.2
HEAT_DILATION = 0.5
SURFACE_TERM = 0.01
ROW_DECAY = 0.6
COLUMN_DECAY = 0.6
PAD = 8


def column_operator(extent):
    position = np.arange(extent)
    distance = np.abs(position[:, None] - position[None, :]).astype(np.float64)
    exact = (COLUMN_DECAY**distance).astype(np.float32)
    high = exact.astype(ml_dtypes.bfloat16)
    low = (exact - high.astype(np.float32)).astype(ml_dtypes.bfloat16)
    return np.block([[high, low], [high, np.zeros_like(low)]])


def kernel(
    nx, ny, tiers, rows, cols,
    t_hbm, u_hbm, v_hbm, lev_hbm, op_ref,
    t_out, u_out, v_out, height_ref,
    tpad, upad, vpad, levint, levpad, tnext, unext, vnext,
    txs, typad, sw, dw, le, lw, ln, ls,
    rr, uu, ww, mm, nn, zz, qq, ss, pp,
    ins_s, ins_r, iew_s, iew_r, iew_c,
    sew_s, sew_r, sns_s, sns_r, ar_s, ar_r,
    in_sem, out_sem, ih_send, ih_recv, sh_send, sh_recv, ar_send, ar_recv,
):
    blocks = rows // BY
    pairs = tiers // 2
    fields = (tpad, upad, vpad)
    lon = lax.axis_index("lon")
    lat = lax.axis_index("lat")
    east = {"lon": lax.rem(lon + 1, nx), "lat": lat}
    west = {"lon": lax.rem(lon + nx - 1, nx), "lat": lat}
    north = {"lon": lon, "lat": lat + 1}
    south = {"lon": lon, "lat": lat - 1}
    has_north = lat < ny - 1
    has_south = lat > 0
    peers = [
        {"lon": lax.rem(lon + dx, nx), "lat": lax.rem(lat + dy, ny)}
        for dy in range(ny)
        for dx in range(nx)
        if dx or dy
    ]
    lane = lax.broadcasted_iota(jnp.int32, (BY, cols), 1)
    sub = lax.broadcasted_iota(jnp.int32, (BY, cols), 0)
    odd = lax.rem(lane, 2) == 1
    first = lane == 0
    last = lane == cols - 1
    thick = [2.0 * (k + 1) / (tiers * (tiers + 1)) for k in range(tiers)]

    loads = [
        pltpu.make_async_copy(src, dst, in_sem.at[i])
        for i, (src, dst) in enumerate(
            [
                (lev_hbm, levint),
                (t_hbm, tpad.at[:, pl.ds(PAD, rows), :]),
                (u_hbm, upad.at[:, pl.ds(PAD, rows), :]),
                (v_hbm, vpad.at[:, pl.ds(PAD, rows), :]),
            ]
        )
    ]
    for load in loads:
        load.start()
    ins_r[...] = jnp.zeros_like(ins_r)
    sns_r[...] = jnp.zeros_like(sns_r)
    barrier = pltpu.get_barrier_semaphore()
    for peer in peers:
        pl.semaphore_signal(barrier, inc=1, device_id=peer, device_id_type=pl.DeviceIdType.MESH)
    for load in loads:
        load.wait()
    levpad[pl.ds(PAD, rows), :] = levint[...].astype(jnp.float32)

    def pack_body(j, carry):
        at = pl.multiple_of(PAD + BY * j, BY)
        here = lax.div(lane, 2) == j
        there = lax.div(lane, 2) == j + cols // 4
        out = []
        for f in range(3):
            for h in range(pairs):
                acc = carry[f * pairs + h]
                a = pltpu.roll(fields[f][2 * h, pl.ds(at, BY), :], 2 * j + 1, 1)
                b = pltpu.roll(fields[f][2 * h + 1, pl.ds(at, BY), :], 2 * j + 1 + cols // 2, 1)
                out.append(jnp.where(here, a, jnp.where(there, b, acc)))
        a = pltpu.roll(levpad[pl.ds(at, BY), :], 2 * j + 1, 1)
        out.append(jnp.where(here, a, carry[3 * pairs]))
        return tuple(out)

    zero = jnp.zeros((BY, cols), jnp.float32)
    packed = lax.fori_loop(0, blocks, pack_body, (zero,) * (3 * pairs + 1))
    for i, value in enumerate(packed):
        iew_s[i] = value
    for side, row in ((0, PAD + rows - 1), (1, PAD)):
        for f in range(3):
            for k in range(tiers):
                ins_s[side, pl.ds(f * tiers + k, 1), :] = fields[f][k, pl.ds(row, 1), :]
        ins_s[side, pl.ds(3 * tiers, BY), :] = jnp.broadcast_to(levpad[pl.ds(row, 1), :], (BY, cols))

    def remote(src, dst, send, recv, device):
        return pltpu.make_async_remote_copy(
            src_ref=src, dst_ref=dst, send_sem=send, recv_sem=recv,
            device_id=device, device_id_type=pl.DeviceIdType.MESH,
        )

    pl.semaphore_wait(barrier, len(peers))

    def exchange(ew_src, ew_dst, ns_src, ns_dst, send, recv):
        to_east = remote(ew_src, ew_dst.at[0], send.at[0], recv.at[0], east)
        to_west = remote(ew_src, ew_dst.at[1], send.at[1], recv.at[1], west)
        to_north = remote(ns_src.at[0], ns_dst.at[0], send.at[2], recv.at[2], north)
        to_south = remote(ns_src.at[1], ns_dst.at[1], send.at[3], recv.at[3], south)

        def start():
            to_east.start()
            to_west.start()
            pl.when(has_north)(to_north.start)
            pl.when(has_south)(to_south.start)

        def wait_recv():
            to_east.wait_recv()
            to_west.wait_recv()
            pl.when(has_south)(to_north.wait_recv)
            pl.when(has_north)(to_south.wait_recv)

        def wait_send():
            to_east.wait_send()
            to_west.wait_send()
            pl.when(has_north)(to_north.wait_send)
            pl.when(has_south)(to_south.wait_send)

        return start, wait_recv, wait_send

    finish = []
    start, wait_recv, wait_send = exchange(iew_s, iew_r, ins_s, ins_r, ih_send, ih_recv)
    start()
    finish.append(wait_send)
    wait_recv()
    for side, row in ((0, PAD - 1), (1, PAD + rows)):
        for f in range(3):
            for k in range(tiers):
                fields[f][k, pl.ds(row, 1), :] = ins_r[side, pl.ds(f * tiers + k, 1), :]
        levpad[pl.ds(row, 1), :] = ins_r[side, pl.ds(3 * tiers, 1), :]

    def combine(from_west, from_east):
        return jnp.where(odd, pltpu.roll(from_west, 1, 1), pltpu.roll(from_east, cols - 1, 1))

    for i in range(3 * pairs + 1):
        iew_c[i] = combine(iew_r[0, i], iew_r[1, i])

    def beside(value, halo):
        e = jnp.where(last, halo, pltpu.roll(value, cols - 1, 1))
        w = jnp.where(first, halo, pltpu.roll(value, 1, 1))
        return e, w

    def field_beside(f, k, j, value):
        shift = cols // 2 - 1 - 2 * j + (0 if k % 2 else cols // 2)
        return beside(value, pltpu.roll(iew_c[f * pairs + k // 2], shift, 1))

    def level_beside(j, value):
        return beside(value, pltpu.roll(iew_c[3 * pairs], cols - 1 - 2 * j, 1))

    def faces(j, at):
        lev = levpad[pl.ds(at, BY), :]
        lev_n = levpad[pl.ds(at + 1, BY), :]
        lev_s = levpad[pl.ds(at - 1, BY), :]
        lev_e, lev_w = level_beside(j, lev)
        return lev, lev_e, lev_w, lev_n, lev_s

    total_rows = rows * ny
    depth_scale = 1.0 / (tiers * (tiers + 1))

    def depth(lev):
        return lev * (lev + 1.0) * depth_scale

    def speed_body(j, _):
        at = pl.multiple_of(PAD + BY * j, BY)
        own = pl.multiple_of(BY * j, BY)
        lev, lev_e, lev_w, lev_n, lev_s = faces(j, at)
        me, mw, mn, ms = [jnp.minimum(lev, o) for o in (lev_e, lev_w, lev_n, lev_s)]
        at_row = (lat * rows + own + sub).astype(jnp.float32)
        f = 2.0 * (at_row + 0.5) / total_rows - 1.0
        de = dw_ = dn = ds = zero
        tx = ty = zero
        for k in range(tiers):
            t = tpad[k, pl.ds(at, BY), :]
            u = upad[k, pl.ds(at, BY), :]
            v = vpad[k, pl.ds(at, BY), :]
            te, tw = field_beside(0, k, j, t)
            ue, uw = field_beside(1, k, j, u)
            ve, vw = field_beside(2, k, j, v)
            tn, ts = tpad[k, pl.ds(at + 1, BY), :], tpad[k, pl.ds(at - 1, BY), :]
            un, us = upad[k, pl.ds(at + 1, BY), :], upad[k, pl.ds(at - 1, BY), :]
            vn, vs = vpad[k, pl.ds(at + 1, BY), :], vpad[k, pl.ds(at - 1, BY), :]
            c = -HEAT_DILATION * thick[k]
            de = de + c * (te - t)
            dw_ = dw_ + c * (t - tw)
            dn = dn + c * (tn - t)
            ds = ds + c * (t - ts)
            ke, kw, kn, ks = me > k, mw > k, mn > k, ms > k
            au = (
                jnp.where(ke, VISCOSITY * (ue - u) - 0.5 * de, 0.0)
                + jnp.where(kw, VISCOSITY * (uw - u) - 0.5 * dw_, 0.0)
                + jnp.where(kn, VISCOSITY * (un - u), 0.0)
                + jnp.where(ks, VISCOSITY * (us - u), 0.0)
            )
            av = (
                jnp.where(ke, VISCOSITY * (ve - v), 0.0)
                + jnp.where(kw, VISCOSITY * (vw - v), 0.0)
                + jnp.where(kn, VISCOSITY * (vn - v) - 0.5 * dn, 0.0)
                + jnp.where(ks, VISCOSITY * (vs - v) - 0.5 * ds, 0.0)
            )
            wet = lev > k
            un_ = jnp.where(wet, u + TIME_STEP * (f * v + au), 0.0)
            vn_ = jnp.where(wet, v + TIME_STEP * (av - f * u), 0.0)
            unext[k, pl.ds(own, BY), :] = un_
            vnext[k, pl.ds(own, BY), :] = vn_
            tx = tx + thick[k] * un_
            ty = ty + thick[k] * vn_
        txs[pl.ds(own, BY), :] = tx
        typad[pl.ds(at, BY), :] = ty
        h = depth(lev)
        link = [
            jnp.where(m > 0, 0.5 * (h + depth(o)), 0.0)
            for m, o in ((me, lev_e), (mw, lev_w), (mn, lev_n), (ms, lev_s))
        ]
        diagonal = SURFACE_TERM + link[0] + link[1] + link[2] + link[3]
        surface = lev > 0
        sw[pl.ds(own, BY), :] = jnp.where(surface, 1.0 / jnp.sqrt(diagonal), 0.0)
        dw[pl.ds(own, BY), :] = jnp.where(surface, diagonal, 0.0)
        for ref, value in zip((le, lw, ln, ls), link):
            ref[pl.ds(own, BY), :] = value
        return 0

    lax.fori_loop(0, blocks, speed_body, 0)
    stores = [
        pltpu.make_async_copy(unext, u_out, out_sem.at[0]),
        pltpu.make_async_copy(vnext, v_out, out_sem.at[1]),
        pltpu.make_async_copy(tnext, t_out, out_sem.at[2]),
    ]
    stores[0].start()
    stores[1].start()

    def tracer_body(j, _):
        at = pl.multiple_of(PAD + BY * j, BY)
        own = pl.multiple_of(BY * j, BY)
        lev, lev_e, lev_w, lev_n, lev_s = faces(j, at)
        me, mw, mn, ms = [jnp.minimum(lev, o) for o in (lev_e, lev_w, lev_n, lev_s)]
        for k in range(tiers):
            t = tpad[k, pl.ds(at, BY), :]
            u = upad[k, pl.ds(at, BY), :]
            v = vpad[k, pl.ds(at, BY), :]
            te, tw = field_beside(0, k, j, t)
            ue, uw = field_beside(1, k, j, u)
            tn, ts = tpad[k, pl.ds(at + 1, BY), :], tpad[k, pl.ds(at - 1, BY), :]
            vn, vs = vpad[k, pl.ds(at + 1, BY), :], vpad[k, pl.ds(at - 1, BY), :]
            flow = (
                jnp.where(me > k, DIFFUSIVITY * (te - t) - 0.25 * (u + ue) * (t + te), 0.0)
                + jnp.where(mw > k, DIFFUSIVITY * (tw - t) + 0.25 * (u + uw) * (t + tw), 0.0)
                + jnp.where(mn > k, DIFFUSIVITY * (tn - t) - 0.25 * (v + vn) * (t + tn), 0.0)
                + jnp.where(ms > k, DIFFUSIVITY * (ts - t) + 0.25 * (v + vs) * (t + ts), 0.0)
            )
            tnext[k, pl.ds(own, BY), :] = jnp.where(lev > k, t + TIME_STEP * flow, 0.0)
        return 0

    def tracer_part(part, parts):
        lax.fori_loop(part * blocks // parts, (part + 1) * blocks // parts, tracer_body, 0)

    def block(j):
        return pl.ds(BY * j, BY)

    def send_surface(phase, ew_ref, ns_ref):
        acc = zero
        for j in range(blocks):
            acc = jnp.where(lax.div(lane, 2) == j, pltpu.roll(ew_ref(j), 2 * j + 1, 1), acc)
        sew_s[phase] = acc
        sns_s[phase, 0] = ns_ref[pl.ds(PAD + rows - 1, 1), :]
        sns_s[phase, 1] = ns_ref[pl.ds(PAD, 1), :]
        start, wait_recv, wait_send = exchange(
            sew_s.at[phase], sew_r.at[phase], sns_s.at[phase], sns_r.at[phase],
            sh_send.at[phase], sh_recv.at[phase],
        )
        start()
        finish.append(wait_send)
        return wait_recv

    def halo_of(phase, ns_ref):
        ns_ref[pl.ds(PAD - 1, 1), :] = sns_r[phase, 0]
        ns_ref[pl.ds(PAD + rows, 1), :] = sns_r[phase, 1]
        comb = combine(sew_r[phase, 0], sew_r[phase, 1])
        return lambda j: pltpu.roll(comb, cols - 1 - 2 * j, 1)

    def pad_block(j, move=0):
        return pl.ds(PAD + BY * j + move, BY)

    def operate(phase, ref, out):
        halo = halo_of(phase, ref)
        for j in range(blocks):
            x = ref[pad_block(j), :]
            e, w = beside(x, halo(j))
            out[block(j), :] = dw[block(j), :] * x - (
                le[block(j), :] * e
                + lw[block(j), :] * w
                + ln[block(j), :] * ref[pad_block(j, 1), :]
                + ls[block(j), :] * ref[pad_block(j, -1), :]
            )

    down = [jnp.where(sub >= d, ROW_DECAY**d, 0.0) for d in (1, 2, 4)]
    up = [jnp.where(sub < BY - d, ROW_DECAY**d, 0.0) for d in (1, 2, 4)]

    def condition(src, dst):
        scaled = sw[...] * src[...]
        high = scaled.astype(jnp.bfloat16)
        low = (scaled - high.astype(jnp.float32)).astype(jnp.bfloat16)
        both = jnp.dot(
            jnp.concatenate([high, low], axis=1), op_ref[...], preferred_element_type=jnp.float32
        )
        across = both[:, :cols] + both[:, cols:]
        for j in range(blocks):
            x = across[BY * j : BY * (j + 1), :]
            f = b = x
            for i, d in enumerate((1, 2, 4)):
                f = f + down[i] * pltpu.roll(f, d, 0)
                b = b + up[i] * pltpu.roll(b, BY - d, 0)
            dst[pad_block(j), :] = sw[block(j), :] * (f + b - x)

    wait = send_surface(0, lambda j: txs[block(j), :], typad)
    tracer_part(0, 5)
    wait()
    halo = halo_of(0, typad)
    for j in range(blocks):
        e, w = beside(txs[block(j), :], halo(j))
        r = -0.5 * ((e - w) + (typad[pad_block(j, 1), :] - typad[pad_block(j, -1), :]))
        rr[block(j), :] = jnp.where(levpad[pad_block(j), :] > 0, r, 0.0)
    condition(rr, uu)
    wait = send_surface(1, lambda j: uu[pad_block(j), :], uu)
    tracer_part(1, 5)
    wait()
    operate(1, uu, ww)

    gamma_old = alpha_old = None
    g = d = zero
    for j in range(blocks):
        g = g + rr[block(j), :] * uu[pad_block(j), :]
        d = d + ww[block(j), :] * uu[pad_block(j), :]
    for it in range(ITERS):
        final = it + 1 == ITERS
        both = jnp.where(odd, d + pltpu.roll(d, cols - 1, 1), g + pltpu.roll(g, cols - 1, 1))
        ar_s[it] = jnp.sum(both, axis=0, keepdims=True)
        copies = [
            remote(ar_s.at[it], ar_r.at[it, i], ar_send.at[it], ar_recv.at[it], peer)
            for i, peer in enumerate(peers)
        ]
        for copy in copies:
            copy.start()
        if not final:
            condition(ww, mm)
            wait = send_surface(2 + it, lambda j: mm[pad_block(j), :], mm)
            tracer_part(2 + it, 5)
            if it + 2 == ITERS:
                stores[2].start()
            wait()
            operate(2 + it, mm, nn)
        pltpu.make_async_copy(ar_r.at[it], ar_r.at[it], ar_recv.at[it]).wait()
        total = ar_s[it]
        for i in range(len(peers)):
            total = total + ar_r[it, i]
        total = jnp.broadcast_to(total, (BY, cols))
        step = 2
        while step < cols:
            total = total + pltpu.roll(total, step, 1)
            step *= 2
        gamma = jnp.where(odd, pltpu.roll(total, 1, 1), total)
        delta = jnp.where(odd, total, pltpu.roll(total, cols - 1, 1))
        if it == 0:
            beta = None
            alpha = gamma / delta
        else:
            beta = gamma / gamma_old
            alpha = gamma / (delta - beta * gamma / alpha_old)
        gamma_old, alpha_old = gamma, alpha
        g = d = zero
        for j in range(blocks):
            u = uu[pad_block(j), :]
            p = u if beta is None else u + beta * pp[block(j), :]
            x = alpha * p if it == 0 else height_ref[block(j), :] + alpha * p
            height_ref[block(j), :] = x
            if final:
                continue
            w = ww[block(j), :]
            z, q, s = nn[block(j), :], mm[pad_block(j), :], w
            if beta is not None:
                z = z + beta * zz[block(j), :]
                q = q + beta * qq[block(j), :]
                s = s + beta * ss[block(j), :]
            if it + 2 < ITERS:
                zz[block(j), :] = z
                qq[block(j), :] = q
                ss[block(j), :] = s
            pp[block(j), :] = p
            r = rr[block(j), :] - alpha * s
            u = u - alpha * q
            w = w - alpha * z
            rr[block(j), :] = r
            uu[pad_block(j), :] = u
            ww[block(j), :] = w
            g = g + r * u
            d = d + w * u

    for wait_send in finish:
        wait_send()
    for it in range(ITERS):
        pltpu.make_async_copy(ar_r.at[it], ar_r.at[it], ar_send.at[it]).wait()
    for store in stores:
        store.wait()


def local(heat_anomaly, zonal_speed, meridional_speed, submerged_tiers_per_site):
    tiers, rows, cols = heat_anomaly.shape
    nx, ny = lax.axis_size("lon"), lax.axis_size("lat")
    operator = jnp.asarray(column_operator(cols))
    f32 = jnp.float32
    field = jax.ShapeDtypeStruct((tiers, rows, cols), f32)
    flat = pltpu.VMEM((rows, cols), f32)
    wide = pltpu.VMEM((rows + 2 * PAD, cols), f32)
    wide3 = pltpu.VMEM((tiers, rows + 2 * PAD, cols), f32)
    full3 = pltpu.VMEM((tiers, rows, cols), f32)
    packs = 3 * (tiers // 2) + 1
    lines = 3 * tiers + BY
    phases = ITERS + 1
    others = nx * ny - 1
    any_spec = pl.BlockSpec(memory_space=pl.ANY)
    vmem_spec = pl.BlockSpec(memory_space=pltpu.VMEM)
    dma = pltpu.SemaphoreType.DMA
    return pl.pallas_call(
        functools.partial(kernel, nx, ny, tiers, rows, cols),
        out_shape=(field, field, field, jax.ShapeDtypeStruct((rows, cols), f32)),
        in_specs=[any_spec] * 4 + [vmem_spec],
        out_specs=(any_spec, any_spec, any_spec, vmem_spec),
        scratch_shapes=[
            wide3, wide3, wide3, pltpu.VMEM((rows, cols), jnp.int32), wide, full3, full3, full3,
            flat, wide, flat, flat, flat, flat, flat, flat,
            flat, wide, flat, wide, flat, flat, flat, flat, flat,
            pltpu.VMEM((2, lines, cols), f32),
            pltpu.VMEM((2, lines, cols), f32),
            pltpu.VMEM((packs, BY, cols), f32),
            pltpu.VMEM((2, packs, BY, cols), f32),
            pltpu.VMEM((packs, BY, cols), f32),
            pltpu.VMEM((phases, BY, cols), f32),
            pltpu.VMEM((phases, 2, BY, cols), f32),
            pltpu.VMEM((phases, 2, 1, cols), f32),
            pltpu.VMEM((phases, 2, 1, cols), f32),
            pltpu.VMEM((ITERS, 1, cols), f32),
            pltpu.VMEM((ITERS, others, 1, cols), f32),
            dma((4,)), dma((3,)), dma((4,)), dma((4,)),
            dma((phases, 4)), dma((phases, 4)), dma((ITERS,)), dma((ITERS,)),
        ],
        compiler_params=pltpu.CompilerParams(
            collective_id=0, has_side_effects=True, vmem_limit_bytes=32 * 1024 * 1024
        ),
        name="ocean_step",
    )(heat_anomaly, zonal_speed, meridional_speed, submerged_tiers_per_site, operator)


def solution(mesh):
    placed = (
        P("groups", "lat", "lon"),
        P("groups", "lat", "lon"),
        P("groups", "lat", "lon"),
        P(("groups", "lat"), "lon"),
    )
    return jax.shard_map(
        local,
        mesh=mesh,
        in_specs=placed,
        out_specs=placed,
        check_vma=False,
    )
```

```python
import functools

import jax
import jax.numpy as jnp
import ml_dtypes
import numpy as np
from jax import lax
from jax.experimental import pallas as pl
from jax.experimental.pallas import tpu as pltpu
from jax.sharding import PartitionSpec as P

BY = 8
ITERS = 4
TIME_STEP = 0.05
DIFFUSIVITY = 0.2
VISCOSITY = 0.2
HEAT_DILATION = 0.5
SURFACE_TERM = 0.01
ROW_DECAY = 0.6
COLUMN_DECAY = 0.6
PAD = 8
CENTRE = 1.2
RADIUS = 1.2
SLOTS = 16


def column_operator(extent):
    position = np.arange(extent)
    distance = np.abs(position[:, None] - position[None, :]).astype(np.float64)
    exact = (COLUMN_DECAY**distance).astype(np.float32)
    high = exact.astype(ml_dtypes.bfloat16)
    low = (exact - high.astype(np.float32)).astype(ml_dtypes.bfloat16)
    return np.block([[high, low], [high, np.zeros_like(low)]])


def kernel(
    nx, ny, tiers, rows, cols,
    t_hbm, u_hbm, v_hbm, lev_hbm, op_ref,
    tnext, unext, vnext, height_ref,
    tpad, upad, vpad, levint, levpad,
    txs, typad, sw, dw, le, lw, ln, ls,
    rr, b0, b1, b2, b3, a0, a1, a2, a3,
    ins_s, ins_r, iew_s, iew_r, iew_c,
    sew_s, sew_r, sns_s, sns_r, ar_s, ar_r,
    in_sem, ih_send, ih_recv, sh_send, sh_recv, ar_send, ar_recv,
):
    blocks = rows // BY
    pairs = tiers // 2
    basis, images = (b0, b1, b2, b3), (a0, a1, a2, a3)
    fields = (tpad, upad, vpad)
    lon = lax.axis_index("lon")
    lat = lax.axis_index("lat")
    east = {"lon": lax.rem(lon + 1, nx), "lat": lat}
    west = {"lon": lax.rem(lon + nx - 1, nx), "lat": lat}
    north = {"lon": lon, "lat": lat + 1}
    south = {"lon": lon, "lat": lat - 1}
    has_north = lat < ny - 1
    has_south = lat > 0
    peers = [
        {"lon": lax.rem(lon + dx, nx), "lat": lax.rem(lat + dy, ny)}
        for dy in range(ny)
        for dx in range(nx)
        if dx or dy
    ]
    lane = lax.broadcasted_iota(jnp.int32, (BY, cols), 1)
    sub = lax.broadcasted_iota(jnp.int32, (BY, cols), 0)
    odd = lax.rem(lane, 2) == 1
    first = lane == 0
    last = lane == cols - 1
    thick = [2.0 * (k + 1) / (tiers * (tiers + 1)) for k in range(tiers)]

    loads = [
        pltpu.make_async_copy(src, dst, in_sem.at[i])
        for i, (src, dst) in enumerate(
            [
                (lev_hbm, levint),
                (t_hbm, tpad.at[:, pl.ds(PAD, rows), :]),
                (u_hbm, upad.at[:, pl.ds(PAD, rows), :]),
                (v_hbm, vpad.at[:, pl.ds(PAD, rows), :]),
            ]
        )
    ]
    for load in loads:
        load.start()
    ins_r[...] = jnp.zeros_like(ins_r)
    sns_r[...] = jnp.zeros_like(sns_r)
    barrier = pltpu.get_barrier_semaphore()
    for peer in peers:
        pl.semaphore_signal(barrier, inc=1, device_id=peer, device_id_type=pl.DeviceIdType.MESH)
    for load in loads:
        load.wait()
    levpad[pl.ds(PAD, rows), :] = levint[...].astype(jnp.float32)

    def pack_body(j, carry):
        at = pl.multiple_of(PAD + BY * j, BY)
        here = lax.div(lane, 2) == j
        there = lax.div(lane, 2) == j + cols // 4
        out = []
        for f in range(3):
            for h in range(pairs):
                acc = carry[f * pairs + h]
                a = pltpu.roll(fields[f][2 * h, pl.ds(at, BY), :], 2 * j + 1, 1)
                b = pltpu.roll(fields[f][2 * h + 1, pl.ds(at, BY), :], 2 * j + 1 + cols // 2, 1)
                out.append(jnp.where(here, a, jnp.where(there, b, acc)))
        a = pltpu.roll(levpad[pl.ds(at, BY), :], 2 * j + 1, 1)
        out.append(jnp.where(here, a, carry[3 * pairs]))
        return tuple(out)

    zero = jnp.zeros((BY, cols), jnp.float32)
    packed = lax.fori_loop(0, blocks, pack_body, (zero,) * (3 * pairs + 1))
    for i, value in enumerate(packed):
        iew_s[i] = value
    for side, row in ((0, PAD + rows - 1), (1, PAD)):
        for f in range(3):
            for k in range(tiers):
                ins_s[side, pl.ds(f * tiers + k, 1), :] = fields[f][k, pl.ds(row, 1), :]
        ins_s[side, pl.ds(3 * tiers, BY), :] = jnp.broadcast_to(levpad[pl.ds(row, 1), :], (BY, cols))

    def remote(src, dst, send, recv, device):
        return pltpu.make_async_remote_copy(
            src_ref=src, dst_ref=dst, send_sem=send, recv_sem=recv,
            device_id=device, device_id_type=pl.DeviceIdType.MESH,
        )

    pl.semaphore_wait(barrier, len(peers))

    def exchange(ew_src, ew_dst, ns_src, ns_dst, send, recv):
        to_east = remote(ew_src, ew_dst.at[0], send.at[0], recv.at[0], east)
        to_west = remote(ew_src, ew_dst.at[1], send.at[1], recv.at[1], west)
        to_north = remote(ns_src.at[0], ns_dst.at[0], send.at[2], recv.at[2], north)
        to_south = remote(ns_src.at[1], ns_dst.at[1], send.at[3], recv.at[3], south)

        def start():
            to_east.start()
            to_west.start()
            pl.when(has_north)(to_north.start)
            pl.when(has_south)(to_south.start)

        def wait_recv():
            to_east.wait_recv()
            to_west.wait_recv()
            pl.when(has_south)(to_north.wait_recv)
            pl.when(has_north)(to_south.wait_recv)

        def wait_send():
            to_east.wait_send()
            to_west.wait_send()
            pl.when(has_north)(to_north.wait_send)
            pl.when(has_south)(to_south.wait_send)

        return start, wait_recv, wait_send

    finish = []
    start, wait_recv, wait_send = exchange(iew_s, iew_r, ins_s, ins_r, ih_send, ih_recv)
    start()
    finish.append(wait_send)
    wait_recv()
    for side, row in ((0, PAD - 1), (1, PAD + rows)):
        for f in range(3):
            for k in range(tiers):
                fields[f][k, pl.ds(row, 1), :] = ins_r[side, pl.ds(f * tiers + k, 1), :]
        levpad[pl.ds(row, 1), :] = ins_r[side, pl.ds(3 * tiers, 1), :]

    def combine(from_west, from_east):
        return jnp.where(odd, pltpu.roll(from_west, 1, 1), pltpu.roll(from_east, cols - 1, 1))

    for i in range(3 * pairs + 1):
        iew_c[i] = combine(iew_r[0, i], iew_r[1, i])

    def beside(value, halo):
        e = jnp.where(last, halo, pltpu.roll(value, cols - 1, 1))
        w = jnp.where(first, halo, pltpu.roll(value, 1, 1))
        return e, w

    def field_beside(f, k, j, value):
        shift = cols // 2 - 1 - 2 * j + (0 if k % 2 else cols // 2)
        return beside(value, pltpu.roll(iew_c[f * pairs + k // 2], shift, 1))

    def level_beside(j, value):
        return beside(value, pltpu.roll(iew_c[3 * pairs], cols - 1 - 2 * j, 1))

    def faces(j, at):
        lev = levpad[pl.ds(at, BY), :]
        lev_n = levpad[pl.ds(at + 1, BY), :]
        lev_s = levpad[pl.ds(at - 1, BY), :]
        lev_e, lev_w = level_beside(j, lev)
        return lev, lev_e, lev_w, lev_n, lev_s

    total_rows = rows * ny
    depth_scale = 1.0 / (tiers * (tiers + 1))

    def depth(lev):
        return lev * (lev + 1.0) * depth_scale

    def speed_body(j, _):
        at = pl.multiple_of(PAD + BY * j, BY)
        own = pl.multiple_of(BY * j, BY)
        lev, lev_e, lev_w, lev_n, lev_s = faces(j, at)
        me, mw, mn, ms = [jnp.minimum(lev, o) for o in (lev_e, lev_w, lev_n, lev_s)]
        at_row = (lat * rows + own + sub).astype(jnp.float32)
        f = 2.0 * (at_row + 0.5) / total_rows - 1.0
        de = dw_ = dn = ds = zero
        tx = ty = zero
        for k in range(tiers):
            t = tpad[k, pl.ds(at, BY), :]
            u = upad[k, pl.ds(at, BY), :]
            v = vpad[k, pl.ds(at, BY), :]
            te, tw = field_beside(0, k, j, t)
            ue, uw = field_beside(1, k, j, u)
            ve, vw = field_beside(2, k, j, v)
            tn, ts = tpad[k, pl.ds(at + 1, BY), :], tpad[k, pl.ds(at - 1, BY), :]
            un, us = upad[k, pl.ds(at + 1, BY), :], upad[k, pl.ds(at - 1, BY), :]
            vn, vs = vpad[k, pl.ds(at + 1, BY), :], vpad[k, pl.ds(at - 1, BY), :]
            c = -HEAT_DILATION * thick[k]
            de = de + c * (te - t)
            dw_ = dw_ + c * (t - tw)
            dn = dn + c * (tn - t)
            ds = ds + c * (t - ts)
            ke, kw, kn, ks = me > k, mw > k, mn > k, ms > k
            au = (
                jnp.where(ke, VISCOSITY * (ue - u) - 0.5 * de, 0.0)
                + jnp.where(kw, VISCOSITY * (uw - u) - 0.5 * dw_, 0.0)
                + jnp.where(kn, VISCOSITY * (un - u), 0.0)
                + jnp.where(ks, VISCOSITY * (us - u), 0.0)
            )
            av = (
                jnp.where(ke, VISCOSITY * (ve - v), 0.0)
                + jnp.where(kw, VISCOSITY * (vw - v), 0.0)
                + jnp.where(kn, VISCOSITY * (vn - v) - 0.5 * dn, 0.0)
                + jnp.where(ks, VISCOSITY * (vs - v) - 0.5 * ds, 0.0)
            )
            wet = lev > k
            un_ = jnp.where(wet, u + TIME_STEP * (f * v + au), 0.0)
            vn_ = jnp.where(wet, v + TIME_STEP * (av - f * u), 0.0)
            unext[k, pl.ds(own, BY), :] = un_
            vnext[k, pl.ds(own, BY), :] = vn_
            tx = tx + thick[k] * un_
            ty = ty + thick[k] * vn_
        txs[pl.ds(own, BY), :] = tx
        typad[pl.ds(at, BY), :] = ty
        h = depth(lev)
        link = [
            jnp.where(m > 0, 0.5 * (h + depth(o)), 0.0)
            for m, o in ((me, lev_e), (mw, lev_w), (mn, lev_n), (ms, lev_s))
        ]
        diagonal = SURFACE_TERM + link[0] + link[1] + link[2] + link[3]
        surface = lev > 0
        sw[pl.ds(own, BY), :] = jnp.where(surface, 1.0 / jnp.sqrt(diagonal), 0.0)
        dw[pl.ds(own, BY), :] = jnp.where(surface, diagonal, 0.0)
        for ref, value in zip((le, lw, ln, ls), link):
            ref[pl.ds(own, BY), :] = value
        return 0

    lax.fori_loop(0, blocks, speed_body, 0)
    def tracer_body(j, _):
        at = pl.multiple_of(PAD + BY * j, BY)
        own = pl.multiple_of(BY * j, BY)
        lev, lev_e, lev_w, lev_n, lev_s = faces(j, at)
        me, mw, mn, ms = [jnp.minimum(lev, o) for o in (lev_e, lev_w, lev_n, lev_s)]
        for k in range(tiers):
            t = tpad[k, pl.ds(at, BY), :]
            u = upad[k, pl.ds(at, BY), :]
            v = vpad[k, pl.ds(at, BY), :]
            te, tw = field_beside(0, k, j, t)
            ue, uw = field_beside(1, k, j, u)
            tn, ts = tpad[k, pl.ds(at + 1, BY), :], tpad[k, pl.ds(at - 1, BY), :]
            vn, vs = vpad[k, pl.ds(at + 1, BY), :], vpad[k, pl.ds(at - 1, BY), :]
            flow = (
                jnp.where(me > k, DIFFUSIVITY * (te - t) - 0.25 * (u + ue) * (t + te), 0.0)
                + jnp.where(mw > k, DIFFUSIVITY * (tw - t) + 0.25 * (u + uw) * (t + tw), 0.0)
                + jnp.where(mn > k, DIFFUSIVITY * (tn - t) - 0.25 * (v + vn) * (t + tn), 0.0)
                + jnp.where(ms > k, DIFFUSIVITY * (ts - t) + 0.25 * (v + vs) * (t + ts), 0.0)
            )
            tnext[k, pl.ds(own, BY), :] = jnp.where(lev > k, t + TIME_STEP * flow, 0.0)
        return 0

    def tracer_part(part, parts):
        lax.fori_loop(part * blocks // parts, (part + 1) * blocks // parts, tracer_body, 0)

    def block(j):
        return pl.ds(BY * j, BY)

    def send_surface(phase, ew_ref, ns_ref):
        acc = zero
        for j in range(blocks):
            acc = jnp.where(lax.div(lane, 2) == j, pltpu.roll(ew_ref(j), 2 * j + 1, 1), acc)
        sew_s[phase] = acc
        sns_s[phase, 0] = ns_ref[pl.ds(PAD + rows - 1, 1), :]
        sns_s[phase, 1] = ns_ref[pl.ds(PAD, 1), :]
        start, wait_recv, wait_send = exchange(
            sew_s.at[phase], sew_r.at[phase], sns_s.at[phase], sns_r.at[phase],
            sh_send.at[phase], sh_recv.at[phase],
        )
        start()
        finish.append(wait_send)
        return wait_recv

    def halo_of(phase, ns_ref):
        ns_ref[pl.ds(PAD - 1, 1), :] = sns_r[phase, 0]
        ns_ref[pl.ds(PAD + rows, 1), :] = sns_r[phase, 1]
        comb = combine(sew_r[phase, 0], sew_r[phase, 1])
        return lambda j: pltpu.roll(comb, cols - 1 - 2 * j, 1)

    def pad_block(j, move=0):
        return pl.ds(PAD + BY * j + move, BY)

    def operate(phase, ref, out):
        halo = halo_of(phase, ref)
        for j in range(blocks):
            x = ref[pad_block(j), :]
            e, w = beside(x, halo(j))
            out[block(j), :] = dw[block(j), :] * x - (
                le[block(j), :] * e
                + lw[block(j), :] * w
                + ln[block(j), :] * ref[pad_block(j, 1), :]
                + ls[block(j), :] * ref[pad_block(j, -1), :]
            )

    down = [jnp.where(sub >= d, ROW_DECAY**d, 0.0) for d in (1, 2, 4)]
    up = [jnp.where(sub < BY - d, ROW_DECAY**d, 0.0) for d in (1, 2, 4)]

    def condition(src, dst, scale=1.0, minus=()):
        scaled = sw[...] * src[...]
        high = scaled.astype(jnp.bfloat16)
        low = (scaled - high.astype(jnp.float32)).astype(jnp.bfloat16)
        both = jnp.dot(
            jnp.concatenate([high, low], axis=1), op_ref[...], preferred_element_type=jnp.float32
        )
        across = both[:, :cols] + both[:, cols:]
        for j in range(blocks):
            x = across[BY * j : BY * (j + 1), :]
            f = b = x
            for i, d in enumerate((1, 2, 4)):
                f = f + down[i] * pltpu.roll(f, d, 0)
                b = b + up[i] * pltpu.roll(b, BY - d, 0)
            y = scale * sw[block(j), :] * (f + b - x)
            for factor, ref in minus:
                y = y - factor * ref[pad_block(j), :]
            dst[pad_block(j), :] = y

    wait = send_surface(0, lambda j: txs[block(j), :], typad)
    tracer_part(0, 5)
    wait()
    halo = halo_of(0, typad)
    for j in range(blocks):
        e, w = beside(txs[block(j), :], halo(j))
        r = -0.5 * ((e - w) + (typad[pad_block(j, 1), :] - typad[pad_block(j, -1), :]))
        rr[block(j), :] = jnp.where(levpad[pad_block(j), :] > 0, r, 0.0)
    def dot(a, b):
        acc = zero
        for j in range(blocks):
            acc = acc + a(j) * b(j)
        return acc

    def at_block(ref):
        return lambda j: ref[block(j), :]

    def at_pad(ref):
        return lambda j: ref[pad_block(j), :]

    sums = {}
    for k in range(ITERS):
        if k == 0:
            condition(rr, basis[0])
        elif k == 1:
            condition(images[0], basis[1], 1.0 / RADIUS, ((CENTRE / RADIUS, basis[0]),))
        else:
            condition(
                images[k - 1], basis[k], 2.0 / RADIUS,
                ((2.0 * CENTRE / RADIUS, basis[k - 1]), (1.0, basis[k - 2])),
            )
        wait = send_surface(k + 1, at_pad(basis[k]), basis[k])
        sums["f", k] = dot(at_block(rr), at_pad(basis[k]))
        for i in range(k):
            sums[i, k] = dot(at_block(images[i]), at_pad(basis[k]))
        if k:
            sums[k - 1, k - 1] = dot(at_block(images[k - 1]), at_pad(basis[k - 1]))
        tracer_part(k + 1, ITERS + 1)
        if k + 1 == ITERS:
            keys = list(sums)
            tiles = [sums[key] for key in keys]
            tiles += [zero] * (SLOTS - len(tiles))
            width = 1
            while len(tiles) > 1:
                upper = lax.rem(lax.div(lane, width), 2) == 1
                half = len(tiles) // 2
                tiles = [
                    jnp.where(
                        upper,
                        tiles[i + half] + pltpu.roll(tiles[i + half], width, 1),
                        tiles[i] + pltpu.roll(tiles[i], cols - width, 1),
                    )
                    for i in range(half)
                ]
                width *= 2
            early = tiles[0]
        wait()
        operate(k + 1, basis[k], images[k])
    late = dot(at_block(images[-1]), at_pad(basis[-1]))
    width = 1
    while width < SLOTS:
        late = late + pltpu.roll(late, width, 1)
        width *= 2
    keys.append((ITERS - 1, ITERS - 1))

    def slot_of(i):
        at, bits = 0, SLOTS // 2
        width = 1
        while bits:
            at += width if i & bits else 0
            width *= 2
            bits //= 2
        return at

    final = slot_of(len(keys) - 1)
    both = jnp.where(lax.rem(lane, SLOTS) == final, late, early)
    ar_s[...] = jnp.sum(both, axis=0, keepdims=True)
    copies = [
        remote(ar_s, ar_r.at[i], ar_send.at[0], ar_recv.at[0], peer) for i, peer in enumerate(peers)
    ]
    for copy in copies:
        copy.start()
    pltpu.make_async_copy(ar_r, ar_r, ar_recv.at[0]).wait()
    total = ar_s[...]
    for i in range(len(peers)):
        total = total + ar_r[i]
    total = jnp.broadcast_to(total, (BY, cols))
    width = SLOTS
    while width < cols:
        total = total + pltpu.roll(total, width, 1)
        width *= 2
    value = {}
    for i, key in enumerate(keys):
        at = slot_of(i)
        value[key] = jnp.broadcast_to(total[:, at : at + 1], (BY, cols))
    gram = {(i, j): value[i, j] for j in range(ITERS) for i in range(j + 1)}
    rhs = [value["f", k] for k in range(ITERS)]
    floor = [1e-6 * gram[i, i] for i in range(ITERS)]
    inverse = []
    for i in range(ITERS):
        pivot = gram[i, i]
        usable = pivot > floor[i]
        inverse.append(jnp.where(usable, 1.0 / jnp.where(usable, pivot, 1.0), 0.0))
        for j in range(i + 1, ITERS):
            factor = gram[i, j] * inverse[i]
            rhs[j] = rhs[j] - factor * rhs[i]
            for k in range(j, ITERS):
                gram[j, k] = gram[j, k] - factor * gram[i, k]
    weights = [None] * ITERS
    for i in reversed(range(ITERS)):
        acc = rhs[i]
        for j in range(i + 1, ITERS):
            acc = acc - gram[i, j] * weights[j]
        weights[i] = acc * inverse[i]
    for j in range(blocks):
        x = weights[0] * basis[0][pad_block(j), :]
        for k in range(1, ITERS):
            x = x + weights[k] * basis[k][pad_block(j), :]
        height_ref[block(j), :] = x

    for wait_send in finish:
        wait_send()
    pltpu.make_async_copy(ar_r, ar_r, ar_send.at[0]).wait()


def write_kernel(*refs):
    sources, targets, sem = refs[:4], refs[4:8], refs[8]
    copies = [
        pltpu.make_async_copy(source, target, sem.at[i])
        for i, (source, target) in enumerate(zip(sources, targets))
    ]
    for copy in copies:
        copy.start()
    for copy in copies:
        copy.wait()


def local(heat_anomaly, zonal_speed, meridional_speed, submerged_tiers_per_site):
    tiers, rows, cols = heat_anomaly.shape
    nx, ny = lax.axis_size("lon"), lax.axis_size("lat")
    operator = jnp.asarray(column_operator(cols))
    f32 = jnp.float32
    field = jax.ShapeDtypeStruct((tiers, rows, cols), f32)
    shapes = (field, field, field, jax.ShapeDtypeStruct((rows, cols), f32))
    flat = pltpu.VMEM((rows, cols), f32)
    wide = pltpu.VMEM((rows + 2 * PAD, cols), f32)
    wide3 = pltpu.VMEM((tiers, rows + 2 * PAD, cols), f32)
    packs = 3 * (tiers // 2) + 1
    lines = 3 * tiers + BY
    phases = ITERS + 1
    others = nx * ny - 1
    any_spec = pl.BlockSpec(memory_space=pl.ANY)
    vmem_spec = pl.BlockSpec(memory_space=pltpu.VMEM)
    dma = pltpu.SemaphoreType.DMA
    results = pl.pallas_call(
        functools.partial(kernel, nx, ny, tiers, rows, cols),
        out_shape=shapes,
        in_specs=[any_spec] * 4 + [vmem_spec],
        out_specs=(vmem_spec,) * 4,
        scratch_shapes=[
            wide3, wide3, wide3, pltpu.VMEM((rows, cols), jnp.int32), wide,
            flat, wide, flat, flat, flat, flat, flat, flat,
            flat, wide, wide, wide, wide, flat, flat, flat, flat,
            pltpu.VMEM((2, lines, cols), f32),
            pltpu.VMEM((2, lines, cols), f32),
            pltpu.VMEM((packs, BY, cols), f32),
            pltpu.VMEM((2, packs, BY, cols), f32),
            pltpu.VMEM((packs, BY, cols), f32),
            pltpu.VMEM((phases, BY, cols), f32),
            pltpu.VMEM((phases, 2, BY, cols), f32),
            pltpu.VMEM((phases, 2, 1, cols), f32),
            pltpu.VMEM((phases, 2, 1, cols), f32),
            pltpu.VMEM((1, cols), f32),
            pltpu.VMEM((others, 1, cols), f32),
            dma((4,)), dma((4,)), dma((4,)),
            dma((phases, 4)), dma((phases, 4)), dma((1,)), dma((1,)),
        ],
        compiler_params=pltpu.CompilerParams(
            collective_id=0, has_side_effects=True, vmem_limit_bytes=60 * 1024 * 1024
        ),
        name="ocean_step",
    )(heat_anomaly, zonal_speed, meridional_speed, submerged_tiers_per_site, operator)
    return pl.pallas_call(
        write_kernel,
        out_shape=shapes,
        in_specs=[vmem_spec] * 4,
        out_specs=(any_spec,) * 4,
        scratch_shapes=[dma((4,))],
        name="write_results",
    )(*results)


def solution(mesh):
    placed = (
        P("groups", "lat", "lon"),
        P("groups", "lat", "lon"),
        P("groups", "lat", "lon"),
        P(("groups", "lat"), "lon"),
    )
    return jax.shard_map(
        local,
        mesh=mesh,
        in_specs=placed,
        out_specs=placed,
        check_vma=False,
    )
```

```python
import functools

import jax
import jax.numpy as jnp
import ml_dtypes
import numpy as np
from jax import lax
from jax.experimental import pallas as pl
from jax.experimental.pallas import tpu as pltpu
from jax.sharding import PartitionSpec as P

BY = 8
ITERS = 4
TIME_STEP = 0.05
DIFFUSIVITY = 0.2
VISCOSITY = 0.2
HEAT_DILATION = 0.5
SURFACE_TERM = 0.01
ROW_DECAY = 0.6
COLUMN_DECAY = 0.6
PAD = 8
CENTRE = 1.2
RADIUS = 1.2
SLOTS = 16


def column_operator(extent):
    position = np.arange(extent)
    distance = np.abs(position[:, None] - position[None, :]).astype(np.float64)
    exact = (COLUMN_DECAY**distance).astype(np.float32)
    high = exact.astype(ml_dtypes.bfloat16)
    low = (exact - high.astype(np.float32)).astype(ml_dtypes.bfloat16)
    return np.block([[high, low], [high, np.zeros_like(low)]])


def kernel(
    nx, ny, tiers, rows, cols,
    t_hbm, u_hbm, v_hbm, lev_hbm, op_ref,
    tnext, unext, vnext, height_ref,
    tpad, upad, vpad, levint, levpad,
    txs, typad, sw, dw, le, lw, ln, ls,
    rr, b0, b1, b2, b3, a0, a1, a2, a3,
    ins_s, ins_r, iew_s, iew_r, iew_c,
    sew_s, sew_r, sns_s, sns_r, ar_s, ar_r,
    in_sem, ih_send, ih_recv, sh_send, sh_recv, ar_send, ar_recv,
):
    blocks = rows // BY
    pairs = tiers // 2
    basis, images = (b0, b1, b2, b3), (a0, a1, a2, a3)
    fields = (tpad, upad, vpad)
    lon = lax.axis_index("lon")
    lat = lax.axis_index("lat")
    east = {"lon": lax.rem(lon + 1, nx), "lat": lat}
    west = {"lon": lax.rem(lon + nx - 1, nx), "lat": lat}
    north = {"lon": lon, "lat": lat + 1}
    south = {"lon": lon, "lat": lat - 1}
    has_north = lat < ny - 1
    has_south = lat > 0
    peers = [
        {"lon": lax.rem(lon + dx, nx), "lat": lax.rem(lat + dy, ny)}
        for dy in range(ny)
        for dx in range(nx)
        if dx or dy
    ]
    lane = lax.broadcasted_iota(jnp.int32, (BY, cols), 1)
    sub = lax.broadcasted_iota(jnp.int32, (BY, cols), 0)
    odd = lax.rem(lane, 2) == 1
    zero = jnp.zeros((BY, cols), jnp.float32)
    first = lane == 0
    last = lane == cols - 1
    thick = [2.0 * (k + 1) / (tiers * (tiers + 1)) for k in range(tiers)]

    loads = [
        pltpu.make_async_copy(src, dst, in_sem.at[i])
        for i, (src, dst) in enumerate(
            [
                (lev_hbm, levint),
                (t_hbm, tpad.at[:, pl.ds(PAD, rows), :]),
                (u_hbm, upad.at[:, pl.ds(PAD, rows), :]),
                (v_hbm, vpad.at[:, pl.ds(PAD, rows), :]),
            ]
        )
    ]
    for load in loads:
        load.start()
    ins_r[...] = jnp.zeros_like(ins_r)
    levpad[pl.ds(0, PAD), :] = zero
    levpad[pl.ds(PAD + rows, PAD), :] = zero
    sns_r[...] = jnp.zeros_like(sns_r)
    barrier = pltpu.get_barrier_semaphore()
    for peer in peers:
        pl.semaphore_signal(barrier, inc=1, device_id=peer, device_id_type=pl.DeviceIdType.MESH)
    for load in loads:
        load.wait()
    levpad[pl.ds(PAD, rows), :] = levint[...].astype(jnp.float32)

    def pack_body(j, carry):
        at = pl.multiple_of(PAD + BY * j, BY)
        here = lax.div(lane, 2) == j
        there = lax.div(lane, 2) == j + cols // 4
        out = []
        for f in range(3):
            for h in range(pairs):
                acc = carry[f * pairs + h]
                a = pltpu.roll(fields[f][2 * h, pl.ds(at, BY), :], 2 * j + 1, 1)
                b = pltpu.roll(fields[f][2 * h + 1, pl.ds(at, BY), :], 2 * j + 1 + cols // 2, 1)
                out.append(jnp.where(here, a, jnp.where(there, b, acc)))
        a = pltpu.roll(levpad[pl.ds(at, BY), :], 2 * j + 1, 1)
        out.append(jnp.where(here, a, carry[3 * pairs]))
        return tuple(out)

    packed = lax.fori_loop(0, blocks, pack_body, (zero,) * (3 * pairs + 1))
    for i, value in enumerate(packed):
        iew_s[i] = value
    for side, row in ((0, PAD + rows - 1), (1, PAD)):
        for f in range(3):
            for k in range(tiers):
                ins_s[side, pl.ds(f * tiers + k, 1), :] = fields[f][k, pl.ds(row, 1), :]
        ins_s[side, pl.ds(3 * tiers, BY), :] = jnp.broadcast_to(levpad[pl.ds(row, 1), :], (BY, cols))

    def remote(src, dst, send, recv, device):
        return pltpu.make_async_remote_copy(
            src_ref=src, dst_ref=dst, send_sem=send, recv_sem=recv,
            device_id=device, device_id_type=pl.DeviceIdType.MESH,
        )

    pl.semaphore_wait(barrier, len(peers))

    def exchange(ew_src, ew_dst, ns_src, ns_dst, send, recv):
        to_east = remote(ew_src, ew_dst.at[0], send.at[0], recv.at[0], east)
        to_west = remote(ew_src, ew_dst.at[1], send.at[1], recv.at[1], west)
        to_north = remote(ns_src.at[0], ns_dst.at[0], send.at[2], recv.at[2], north)
        to_south = remote(ns_src.at[1], ns_dst.at[1], send.at[3], recv.at[3], south)

        def start():
            to_east.start()
            to_west.start()
            pl.when(has_north)(to_north.start)
            pl.when(has_south)(to_south.start)

        def wait_recv():
            to_east.wait_recv()
            to_west.wait_recv()
            pl.when(has_south)(to_north.wait_recv)
            pl.when(has_north)(to_south.wait_recv)

        def wait_send():
            to_east.wait_send()
            to_west.wait_send()
            pl.when(has_north)(to_north.wait_send)
            pl.when(has_south)(to_south.wait_send)

        return start, wait_recv, wait_send

    finish = []
    start, wait_recv, wait_send = exchange(iew_s, iew_r, ins_s, ins_r, ih_send, ih_recv)
    start()
    finish.append(wait_send)
    total_rows = rows * ny
    depth_scale = 1.0 / (tiers * (tiers + 1))
    edge = first | last
    high_half = lane >= cols // 2

    def depth(lev):
        return lev * (lev + 1.0) * depth_scale

    def inner_faces(at):
        lev = levpad[pl.ds(at, BY), :]
        lev_e = jnp.where(last, 0.0, pltpu.roll(lev, cols - 1, 1))
        me = jnp.minimum(lev, lev_e)
        mn = jnp.minimum(lev, levpad[pl.ds(at + 1, BY), :])
        ms = jnp.minimum(lev, levpad[pl.ds(at - 1, BY), :])
        return lev, me, mn, ms

    def east_of(value):
        return pltpu.roll(value, cols - 1, 1)

    def west_of(value):
        return pltpu.roll(value, 1, 1)

    def speed_body(j, carry):
        at = pl.multiple_of(PAD + BY * j, BY)
        own = pl.multiple_of(BY * j, BY)
        lev, me, mn, ms = inner_faces(at)
        at_row = (lat * rows + own + sub).astype(jnp.float32)
        f = 2.0 * (at_row + 0.5) / total_rows - 1.0
        de = dn = ds = zero
        tx = ty = zero
        for k in range(tiers):
            t = tpad[k, pl.ds(at, BY), :]
            u = upad[k, pl.ds(at, BY), :]
            v = vpad[k, pl.ds(at, BY), :]
            tn, ts = tpad[k, pl.ds(at + 1, BY), :], tpad[k, pl.ds(at - 1, BY), :]
            un, us = upad[k, pl.ds(at + 1, BY), :], upad[k, pl.ds(at - 1, BY), :]
            vn, vs = vpad[k, pl.ds(at + 1, BY), :], vpad[k, pl.ds(at - 1, BY), :]
            c = -0.5 * HEAT_DILATION * thick[k]
            de = de + c * (east_of(t) - t)
            dn = dn + c * (tn - t)
            ds = ds + c * (t - ts)
            ke, kn, ks = me > k, mn > k, ms > k
            gu = jnp.where(ke, VISCOSITY * (east_of(u) - u), 0.0)
            gv = jnp.where(ke, VISCOSITY * (east_of(v) - v), 0.0)
            gp = jnp.where(ke, de, 0.0)
            au = (
                (gu - gp)
                - west_of(gu + gp)
                + jnp.where(kn, VISCOSITY * (un - u), 0.0)
                + jnp.where(ks, VISCOSITY * (us - u), 0.0)
            )
            av = (
                gv
                - west_of(gv)
                + jnp.where(kn, VISCOSITY * (vn - v) - dn, 0.0)
                + jnp.where(ks, VISCOSITY * (vs - v) - ds, 0.0)
            )
            wet = lev > k
            un_ = jnp.where(wet, u + TIME_STEP * (f * v + au), 0.0)
            vn_ = jnp.where(wet, v + TIME_STEP * (av - f * u), 0.0)
            unext[k, pl.ds(own, BY), :] = un_
            vnext[k, pl.ds(own, BY), :] = vn_
            tx = tx + thick[k] * un_
            ty = ty + thick[k] * vn_
        txs[pl.ds(own, BY), :] = tx
        typad[pl.ds(at, BY), :] = ty
        return carry

    lax.fori_loop(1, blocks - 1, speed_body, 0)
    wait_recv()
    for side, row in ((0, PAD - 1), (1, PAD + rows)):
        for f in range(3):
            for k in range(tiers):
                fields[f][k, pl.ds(row, 1), :] = ins_r[side, pl.ds(f * tiers + k, 1), :]
        levpad[pl.ds(row, 1), :] = ins_r[side, pl.ds(3 * tiers, 1), :]

    def combine(from_west, from_east):
        return jnp.where(odd, pltpu.roll(from_west, 1, 1), pltpu.roll(from_east, cols - 1, 1))

    lax.fori_loop(0, 2, lambda i, carry: speed_body(i * (blocks - 1), carry), 0)

    lev_own = iew_s[3 * pairs]
    lev_halo = combine(iew_r[0, 3 * pairs], iew_r[1, 3 * pairs])
    iew_c[3 * pairs] = lev_halo
    face = jnp.minimum(lev_own, lev_halo)
    face = face + pltpu.roll(face, cols // 2, 1)
    outward = jnp.where(odd, -1.0, 1.0)
    load = tx_edge = ty_edge = zero
    for h in range(pairs):
        own_, halo_ = [], []
        for f in range(3):
            own_.append(iew_s[f * pairs + h])
            halo_.append(combine(iew_r[0, f * pairs + h], iew_r[1, f * pairs + h]))
        (t, u, v), (th, uh, vh) = own_, halo_
        weight = jnp.where(high_half, thick[2 * h + 1], thick[2 * h])
        wet = face > jnp.where(high_half, 2.0 * h + 1.0, 2.0 * h)
        part = (-0.5 * HEAT_DILATION) * weight * (th - t)
        other = pltpu.roll(part, cols // 2, 1)
        slope = load + part + jnp.where(high_half, other, 0.0)
        load = load + part + other
        cu = TIME_STEP * jnp.where(wet, VISCOSITY * (uh - u) - outward * slope, 0.0)
        cv = TIME_STEP * jnp.where(wet, VISCOSITY * (vh - v), 0.0)
        ct = TIME_STEP * jnp.where(
            wet, DIFFUSIVITY * (th - t) - outward * (0.25 * (u + uh) * (t + th)), 0.0
        )
        iew_c[h] = ct
        iew_c[pairs + h] = cu
        iew_c[2 * pairs + h] = cv
        tx_edge = tx_edge + weight * cu
        ty_edge = ty_edge + weight * cv
    tx_edge = tx_edge + pltpu.roll(tx_edge, cols // 2, 1)
    ty_edge = ty_edge + pltpu.roll(ty_edge, cols // 2, 1)
    for j in range(blocks):
        here, shift = pl.ds(BY * j, BY), cols - 1 - 2 * j
        pad = pl.ds(PAD + BY * j, BY)
        txs[here, :] = txs[here, :] + jnp.where(edge, pltpu.roll(tx_edge, shift, 1), 0.0)
        typad[pad, :] = typad[pad, :] + jnp.where(edge, pltpu.roll(ty_edge, shift, 1), 0.0)

    def beside(value, halo):
        e = jnp.where(last, halo, pltpu.roll(value, cols - 1, 1))
        w = jnp.where(first, halo, pltpu.roll(value, 1, 1))
        return e, w

    def coefficients():
        for j in range(blocks):
            at, here = PAD + BY * j, pl.ds(BY * j, BY)
            lev = levpad[pl.ds(at, BY), :]
            lev_e, lev_w = beside(lev, pltpu.roll(iew_c[3 * pairs], cols - 1 - 2 * j, 1))
            lev_n = levpad[pl.ds(at + 1, BY), :]
            lev_s = levpad[pl.ds(at - 1, BY), :]
            h = depth(lev)
            surface = lev > 0
            link = [
                jnp.where(surface & (o > 0), 0.5 * (h + depth(o)), 0.0)
                for o in (lev_e, lev_w, lev_n, lev_s)
            ]
            diagonal = SURFACE_TERM + link[0] + link[1] + link[2] + link[3]
            sw[here, :] = jnp.where(surface, 1.0 / jnp.sqrt(diagonal), 0.0)
            dw[here, :] = jnp.where(surface, diagonal, 0.0)
            for ref, value in zip((le, lw, ln, ls), link):
                ref[here, :] = value

    def tracer_body(j, carry):
        at = pl.multiple_of(PAD + BY * j, BY)
        own = pl.multiple_of(BY * j, BY)
        lev, me, mn, ms = inner_faces(at)
        for k in range(tiers):
            t = tpad[k, pl.ds(at, BY), :]
            u = upad[k, pl.ds(at, BY), :]
            v = vpad[k, pl.ds(at, BY), :]
            te, ue = east_of(t), east_of(u)
            tn, ts = tpad[k, pl.ds(at + 1, BY), :], tpad[k, pl.ds(at - 1, BY), :]
            vn, vs = vpad[k, pl.ds(at + 1, BY), :], vpad[k, pl.ds(at - 1, BY), :]
            ge = jnp.where(me > k, DIFFUSIVITY * (te - t) - 0.25 * (u + ue) * (t + te), 0.0)
            flow = (
                (ge - west_of(ge))
                + jnp.where(mn > k, DIFFUSIVITY * (tn - t) - 0.25 * (v + vn) * (t + tn), 0.0)
                + jnp.where(ms > k, DIFFUSIVITY * (ts - t) + 0.25 * (v + vs) * (t + ts), 0.0)
            )
            shift = cols // 2 - 1 - 2 * j + (0 if k % 2 else cols // 2)
            ct, cu, cv = [
                jnp.where(edge, pltpu.roll(iew_c[f * pairs + k // 2], shift, 1), 0.0)
                for f in range(3)
            ]
            here = pl.ds(own, BY)
            tnext[k, here, :] = jnp.where(lev > k, t + TIME_STEP * flow, 0.0) + ct
            unext[k, here, :] = unext[k, here, :] + cu
            vnext[k, here, :] = vnext[k, here, :] + cv
        return carry

    def tracer_part(part, parts):
        lax.fori_loop(part * blocks // parts, (part + 1) * blocks // parts, tracer_body, 0)

    def block(j):
        return pl.ds(BY * j, BY)

    def send_surface(phase, ew_ref, ns_ref):
        acc = zero
        for j in range(blocks):
            acc = jnp.where(lax.div(lane, 2) == j, pltpu.roll(ew_ref(j), 2 * j + 1, 1), acc)
        sew_s[phase] = acc
        sns_s[phase, 0] = ns_ref[pl.ds(PAD + rows - 1, 1), :]
        sns_s[phase, 1] = ns_ref[pl.ds(PAD, 1), :]
        start, wait_recv, wait_send = exchange(
            sew_s.at[phase], sew_r.at[phase], sns_s.at[phase], sns_r.at[phase],
            sh_send.at[phase], sh_recv.at[phase],
        )
        start()
        finish.append(wait_send)
        return wait_recv

    def halo_of(phase, ns_ref):
        ns_ref[pl.ds(PAD - 1, 1), :] = sns_r[phase, 0]
        ns_ref[pl.ds(PAD + rows, 1), :] = sns_r[phase, 1]
        comb = combine(sew_r[phase, 0], sew_r[phase, 1])
        return lambda j: pltpu.roll(comb, cols - 1 - 2 * j, 1)

    def pad_block(j, move=0):
        return pl.ds(PAD + BY * j + move, BY)

    def operate(phase, ref, out):
        halo = halo_of(phase, ref)
        for j in range(blocks):
            x = ref[pad_block(j), :]
            e, w = beside(x, halo(j))
            out[block(j), :] = dw[block(j), :] * x - (
                le[block(j), :] * e
                + lw[block(j), :] * w
                + ln[block(j), :] * ref[pad_block(j, 1), :]
                + ls[block(j), :] * ref[pad_block(j, -1), :]
            )

    down = [jnp.where(sub >= d, ROW_DECAY**d, 0.0) for d in (1, 2, 4)]
    up = [jnp.where(sub < BY - d, ROW_DECAY**d, 0.0) for d in (1, 2, 4)]

    def condition(src, dst, scale=1.0, minus=()):
        scaled = sw[...] * src[...]
        high = scaled.astype(jnp.bfloat16)
        low = (scaled - high.astype(jnp.float32)).astype(jnp.bfloat16)
        both = jnp.dot(
            jnp.concatenate([high, low], axis=1), op_ref[...], preferred_element_type=jnp.float32
        )
        across = both[:, :cols] + both[:, cols:]
        for j in range(blocks):
            x = across[BY * j : BY * (j + 1), :]
            f = b = x
            for i, d in enumerate((1, 2, 4)):
                f = f + down[i] * pltpu.roll(f, d, 0)
                b = b + up[i] * pltpu.roll(b, BY - d, 0)
            y = scale * sw[block(j), :] * (f + b - x)
            for factor, ref in minus:
                y = y - factor * ref[pad_block(j), :]
            dst[pad_block(j), :] = y

    wait = send_surface(0, lambda j: txs[block(j), :], typad)
    coefficients()
    wait()
    halo = halo_of(0, typad)
    for j in range(blocks):
        e, w = beside(txs[block(j), :], halo(j))
        r = -0.5 * ((e - w) + (typad[pad_block(j, 1), :] - typad[pad_block(j, -1), :]))
        rr[block(j), :] = jnp.where(levpad[pad_block(j), :] > 0, r, 0.0)
    def dot(a, b):
        acc = zero
        for j in range(blocks):
            acc = acc + a(j) * b(j)
        return acc

    def at_block(ref):
        return lambda j: ref[block(j), :]

    def at_pad(ref):
        return lambda j: ref[pad_block(j), :]

    sums = {}
    for k in range(ITERS):
        if k == 0:
            condition(rr, basis[0])
        elif k == 1:
            condition(images[0], basis[1], 1.0 / RADIUS, ((CENTRE / RADIUS, basis[0]),))
        else:
            condition(
                images[k - 1], basis[k], 2.0 / RADIUS,
                ((2.0 * CENTRE / RADIUS, basis[k - 1]), (1.0, basis[k - 2])),
            )
        wait = send_surface(k + 1, at_pad(basis[k]), basis[k])
        sums["f", k] = dot(at_block(rr), at_pad(basis[k]))
        for i in range(k):
            sums[i, k] = dot(at_block(images[i]), at_pad(basis[k]))
        if k:
            sums[k - 1, k - 1] = dot(at_block(images[k - 1]), at_pad(basis[k - 1]))
        tracer_part(k, ITERS)
        if k + 1 == ITERS:
            keys = list(sums)
            tiles = [sums[key] for key in keys]
            tiles += [zero] * (SLOTS - len(tiles))
            width = 1
            while len(tiles) > 1:
                upper = lax.rem(lax.div(lane, width), 2) == 1
                half = len(tiles) // 2
                tiles = [
                    jnp.where(
                        upper,
                        tiles[i + half] + pltpu.roll(tiles[i + half], width, 1),
                        tiles[i] + pltpu.roll(tiles[i], cols - width, 1),
                    )
                    for i in range(half)
                ]
                width *= 2
            early = tiles[0]
        wait()
        operate(k + 1, basis[k], images[k])
    late = dot(at_block(images[-1]), at_pad(basis[-1]))
    width = 1
    while width < SLOTS:
        late = late + pltpu.roll(late, width, 1)
        width *= 2
    keys.append((ITERS - 1, ITERS - 1))

    def slot_of(i):
        at, bits = 0, SLOTS // 2
        width = 1
        while bits:
            at += width if i & bits else 0
            width *= 2
            bits //= 2
        return at

    final = slot_of(len(keys) - 1)
    both = jnp.where(lax.rem(lane, SLOTS) == final, late, early)
    ar_s[...] = jnp.sum(both, axis=0, keepdims=True)
    copies = [
        remote(ar_s, ar_r.at[i], ar_send.at[0], ar_recv.at[0], peer) for i, peer in enumerate(peers)
    ]
    for copy in copies:
        copy.start()
    pltpu.make_async_copy(ar_r, ar_r, ar_recv.at[0]).wait()
    total = ar_s[...]
    for i in range(len(peers)):
        total = total + ar_r[i]
    total = jnp.broadcast_to(total, (BY, cols))
    width = SLOTS
    while width < cols:
        total = total + pltpu.roll(total, width, 1)
        width *= 2
    value = {}
    for i, key in enumerate(keys):
        at = slot_of(i)
        value[key] = jnp.broadcast_to(total[:, at : at + 1], (BY, cols))
    gram = {(i, j): value[i, j] for j in range(ITERS) for i in range(j + 1)}
    rhs = [value["f", k] for k in range(ITERS)]
    floor = [1e-6 * gram[i, i] for i in range(ITERS)]
    inverse = []
    for i in range(ITERS):
        pivot = gram[i, i]
        usable = pivot > floor[i]
        inverse.append(jnp.where(usable, 1.0 / jnp.where(usable, pivot, 1.0), 0.0))
        for j in range(i + 1, ITERS):
            factor = gram[i, j] * inverse[i]
            rhs[j] = rhs[j] - factor * rhs[i]
            for k in range(j, ITERS):
                gram[j, k] = gram[j, k] - factor * gram[i, k]
    weights = [None] * ITERS
    for i in reversed(range(ITERS)):
        acc = rhs[i]
        for j in range(i + 1, ITERS):
            acc = acc - gram[i, j] * weights[j]
        weights[i] = acc * inverse[i]
    for j in range(blocks):
        x = weights[0] * basis[0][pad_block(j), :]
        for k in range(1, ITERS):
            x = x + weights[k] * basis[k][pad_block(j), :]
        height_ref[block(j), :] = x

    for wait_send in finish:
        wait_send()
    pltpu.make_async_copy(ar_r, ar_r, ar_send.at[0]).wait()


def write_kernel(*refs):
    sources, targets, sem = refs[:4], refs[4:8], refs[8]
    copies = [
        pltpu.make_async_copy(source, target, sem.at[i])
        for i, (source, target) in enumerate(zip(sources, targets))
    ]
    for copy in copies:
        copy.start()
    for copy in copies:
        copy.wait()


def local(heat_anomaly, zonal_speed, meridional_speed, submerged_tiers_per_site):
    tiers, rows, cols = heat_anomaly.shape
    nx, ny = lax.axis_size("lon"), lax.axis_size("lat")
    operator = jnp.asarray(column_operator(cols))
    f32 = jnp.float32
    field = jax.ShapeDtypeStruct((tiers, rows, cols), f32)
    shapes = (field, field, field, jax.ShapeDtypeStruct((rows, cols), f32))
    flat = pltpu.VMEM((rows, cols), f32)
    wide = pltpu.VMEM((rows + 2 * PAD, cols), f32)
    wide3 = pltpu.VMEM((tiers, rows + 2 * PAD, cols), f32)
    packs = 3 * (tiers // 2) + 1
    lines = 3 * tiers + BY
    phases = ITERS + 1
    others = nx * ny - 1
    any_spec = pl.BlockSpec(memory_space=pl.ANY)
    vmem_spec = pl.BlockSpec(memory_space=pltpu.VMEM)
    dma = pltpu.SemaphoreType.DMA
    results = pl.pallas_call(
        functools.partial(kernel, nx, ny, tiers, rows, cols),
        out_shape=shapes,
        in_specs=[any_spec] * 4 + [vmem_spec],
        out_specs=(vmem_spec,) * 4,
        scratch_shapes=[
            wide3, wide3, wide3, pltpu.VMEM((rows, cols), jnp.int32), wide,
            flat, wide, flat, flat, flat, flat, flat, flat,
            flat, wide, wide, wide, wide, flat, flat, flat, flat,
            pltpu.VMEM((2, lines, cols), f32),
            pltpu.VMEM((2, lines, cols), f32),
            pltpu.VMEM((packs, BY, cols), f32),
            pltpu.VMEM((2, packs, BY, cols), f32),
            pltpu.VMEM((packs, BY, cols), f32),
            pltpu.VMEM((phases, BY, cols), f32),
            pltpu.VMEM((phases, 2, BY, cols), f32),
            pltpu.VMEM((phases, 2, 1, cols), f32),
            pltpu.VMEM((phases, 2, 1, cols), f32),
            pltpu.VMEM((1, cols), f32),
            pltpu.VMEM((others, 1, cols), f32),
            dma((4,)), dma((4,)), dma((4,)),
            dma((phases, 4)), dma((phases, 4)), dma((1,)), dma((1,)),
        ],
        compiler_params=pltpu.CompilerParams(
            collective_id=0, has_side_effects=True, vmem_limit_bytes=60 * 1024 * 1024
        ),
        name="ocean_step",
    )(heat_anomaly, zonal_speed, meridional_speed, submerged_tiers_per_site, operator)
    return pl.pallas_call(
        write_kernel,
        out_shape=shapes,
        in_specs=[vmem_spec] * 4,
        out_specs=(any_spec,) * 4,
        scratch_shapes=[dma((4,))],
        name="write_results",
    )(*results)


def solution(mesh):
    placed = (
        P("groups", "lat", "lon"),
        P("groups", "lat", "lon"),
        P("groups", "lat", "lon"),
        P(("groups", "lat"), "lon"),
    )
    return jax.shard_map(
        local,
        mesh=mesh,
        in_specs=placed,
        out_specs=placed,
        check_vma=False,
    )
```

```python
import functools

import jax
import jax.numpy as jnp
import ml_dtypes
import numpy as np
from jax import lax
from jax.experimental import pallas as pl
from jax.experimental.pallas import tpu as pltpu
from jax.sharding import PartitionSpec as P

BY = 8
ITERS = 4
TIME_STEP = 0.05
DIFFUSIVITY = 0.2
VISCOSITY = 0.2
HEAT_DILATION = 0.5
SURFACE_TERM = 0.01
ROW_DECAY = 0.6
COLUMN_DECAY = 0.6
PAD = 8
CENTRE = 1.2
RADIUS = 1.2
SLOTS = 16


def column_operator(extent):
    position = np.arange(extent)
    distance = np.abs(position[:, None] - position[None, :]).astype(np.float64)
    exact = (COLUMN_DECAY**distance).astype(np.float32)
    high = exact.astype(ml_dtypes.bfloat16)
    low = (exact - high.astype(np.float32)).astype(ml_dtypes.bfloat16)
    return np.block([[high, low], [high, np.zeros_like(low)]])


def kernel(
    nx, ny, tiers, rows, cols,
    t_hbm, u_hbm, v_hbm, lev_hbm, op_ref,
    tnext, unext, vnext, height_ref,
    tpad, upad, vpad, levint, levpad,
    txs, typad, sw, dw, le, lw, ln, ls,
    rr, b0, b1, b2, b3, a0, a1, a2, a3,
    ins_s, ins_r, iew_s, iew_r, iew_c,
    sew_s, sew_r, sns_s, sns_r, ar_s, ar_r,
    in_sem, ih_send, ih_recv, sh_send, sh_recv, ar_send, ar_recv,
):
    blocks = rows // BY
    pairs = tiers // 2
    basis, images = (b0, b1, b2, b3), (a0, a1, a2, a3)
    fields = (tpad, upad, vpad)
    lon = lax.axis_index("lon")
    lat = lax.axis_index("lat")
    east = {"lon": lax.rem(lon + 1, nx), "lat": lat}
    west = {"lon": lax.rem(lon + nx - 1, nx), "lat": lat}
    north = {"lon": lon, "lat": lat + 1}
    south = {"lon": lon, "lat": lat - 1}
    has_north = lat < ny - 1
    has_south = lat > 0
    peers = [
        {"lon": lax.rem(lon + dx, nx), "lat": lax.rem(lat + dy, ny)}
        for dy in range(ny)
        for dx in range(nx)
        if dx or dy
    ]
    lane = lax.broadcasted_iota(jnp.int32, (BY, cols), 1)
    sub = lax.broadcasted_iota(jnp.int32, (BY, cols), 0)
    odd = lax.rem(lane, 2) == 1
    zero = jnp.zeros((BY, cols), jnp.float32)
    first = lane == 0
    last = lane == cols - 1
    thick = [2.0 * (k + 1) / (tiers * (tiers + 1)) for k in range(tiers)]

    loads = [
        pltpu.make_async_copy(src, dst, in_sem.at[i])
        for i, (src, dst) in enumerate(
            [
                (lev_hbm, levint),
                (t_hbm, tpad.at[:, pl.ds(PAD, rows), :]),
                (u_hbm, upad.at[:, pl.ds(PAD, rows), :]),
                (v_hbm, vpad.at[:, pl.ds(PAD, rows), :]),
            ]
        )
    ]
    for load in loads:
        load.start()
    ins_r[...] = jnp.zeros_like(ins_r)
    levpad[pl.ds(0, PAD), :] = zero
    levpad[pl.ds(PAD + rows, PAD), :] = zero
    sns_r[...] = jnp.zeros_like(sns_r)
    barrier = pltpu.get_barrier_semaphore()
    for peer in peers:
        pl.semaphore_signal(barrier, inc=1, device_id=peer, device_id_type=pl.DeviceIdType.MESH)
    for load in loads:
        load.wait()
    levpad[pl.ds(PAD, rows), :] = levint[...].astype(jnp.float32)

    def pack_body(j, carry):
        at = pl.multiple_of(PAD + BY * j, BY)
        here = lax.div(lane, 2) == j
        there = lax.div(lane, 2) == j + cols // 4
        out = []
        for f in range(3):
            for h in range(pairs):
                acc = carry[f * pairs + h]
                a = pltpu.roll(fields[f][2 * h, pl.ds(at, BY), :], 2 * j + 1, 1)
                b = pltpu.roll(fields[f][2 * h + 1, pl.ds(at, BY), :], 2 * j + 1 + cols // 2, 1)
                out.append(jnp.where(here, a, jnp.where(there, b, acc)))
        a = pltpu.roll(levpad[pl.ds(at, BY), :], 2 * j + 1, 1)
        out.append(jnp.where(here, a, carry[3 * pairs]))
        return tuple(out)

    packed = lax.fori_loop(0, blocks, pack_body, (zero,) * (3 * pairs + 1), unroll=8)
    for i, value in enumerate(packed):
        iew_s[i] = value
    for side, row in ((0, PAD + rows - 1), (1, PAD)):
        for f in range(3):
            for k in range(tiers):
                ins_s[side, pl.ds(f * tiers + k, 1), :] = fields[f][k, pl.ds(row, 1), :]
        ins_s[side, pl.ds(3 * tiers, BY), :] = jnp.broadcast_to(levpad[pl.ds(row, 1), :], (BY, cols))

    def remote(src, dst, send, recv, device):
        return pltpu.make_async_remote_copy(
            src_ref=src, dst_ref=dst, send_sem=send, recv_sem=recv,
            device_id=device, device_id_type=pl.DeviceIdType.MESH,
        )

    pl.semaphore_wait(barrier, len(peers))

    def exchange(ew_src, ew_dst, ns_src, ns_dst, send, recv):
        to_east = remote(ew_src, ew_dst.at[0], send.at[0], recv.at[0], east)
        to_west = remote(ew_src, ew_dst.at[1], send.at[1], recv.at[1], west)
        to_north = remote(ns_src.at[0], ns_dst.at[0], send.at[2], recv.at[2], north)
        to_south = remote(ns_src.at[1], ns_dst.at[1], send.at[3], recv.at[3], south)

        def start():
            to_east.start()
            to_west.start()
            pl.when(has_north)(to_north.start)
            pl.when(has_south)(to_south.start)

        def wait_recv():
            to_east.wait_recv()
            to_west.wait_recv()
            pl.when(has_south)(to_north.wait_recv)
            pl.when(has_north)(to_south.wait_recv)

        def wait_send():
            to_east.wait_send()
            to_west.wait_send()
            pl.when(has_north)(to_north.wait_send)
            pl.when(has_south)(to_south.wait_send)

        return start, wait_recv, wait_send

    finish = []
    start, wait_recv, wait_send = exchange(iew_s, iew_r, ins_s, ins_r, ih_send, ih_recv)
    start()
    finish.append(wait_send)
    total_rows = rows * ny
    depth_scale = 1.0 / (tiers * (tiers + 1))
    edge = first | last
    high_half = lane >= cols // 2

    def depth(lev):
        return lev * (lev + 1.0) * depth_scale

    def inner_faces(at):
        lev = levpad[pl.ds(at, BY), :]
        lev_e = jnp.where(last, 0.0, pltpu.roll(lev, cols - 1, 1))
        me = jnp.minimum(lev, lev_e)
        mn = jnp.minimum(lev, levpad[pl.ds(at + 1, BY), :])
        ms = jnp.minimum(lev, levpad[pl.ds(at - 1, BY), :])
        return lev, me, mn, ms

    def east_of(value):
        return pltpu.roll(value, cols - 1, 1)

    def west_of(value):
        return pltpu.roll(value, 1, 1)

    def speed_body(j, carry):
        at = pl.multiple_of(PAD + BY * j, BY)
        own = pl.multiple_of(BY * j, BY)
        lev, me, mn, ms = inner_faces(at)
        at_row = (lat * rows + own + sub).astype(jnp.float32)
        f = 2.0 * (at_row + 0.5) / total_rows - 1.0
        de = dn = ds = zero
        tx = ty = zero
        for k in range(tiers):
            t = tpad[k, pl.ds(at, BY), :]
            u = upad[k, pl.ds(at, BY), :]
            v = vpad[k, pl.ds(at, BY), :]
            tn, ts = tpad[k, pl.ds(at + 1, BY), :], tpad[k, pl.ds(at - 1, BY), :]
            un, us = upad[k, pl.ds(at + 1, BY), :], upad[k, pl.ds(at - 1, BY), :]
            vn, vs = vpad[k, pl.ds(at + 1, BY), :], vpad[k, pl.ds(at - 1, BY), :]
            c = -0.5 * HEAT_DILATION * thick[k]
            de = de + c * (east_of(t) - t)
            dn = dn + c * (tn - t)
            ds = ds + c * (t - ts)
            ke, kn, ks = me > k, mn > k, ms > k
            gu = jnp.where(ke, VISCOSITY * (east_of(u) - u), 0.0)
            gv = jnp.where(ke, VISCOSITY * (east_of(v) - v), 0.0)
            gp = jnp.where(ke, de, 0.0)
            au = (
                (gu - gp)
                - west_of(gu + gp)
                + jnp.where(kn, VISCOSITY * (un - u), 0.0)
                + jnp.where(ks, VISCOSITY * (us - u), 0.0)
            )
            av = (
                gv
                - west_of(gv)
                + jnp.where(kn, VISCOSITY * (vn - v) - dn, 0.0)
                + jnp.where(ks, VISCOSITY * (vs - v) - ds, 0.0)
            )
            wet = lev > k
            un_ = jnp.where(wet, u + TIME_STEP * (f * v + au), 0.0)
            vn_ = jnp.where(wet, v + TIME_STEP * (av - f * u), 0.0)
            unext[k, pl.ds(own, BY), :] = un_
            vnext[k, pl.ds(own, BY), :] = vn_
            tx = tx + thick[k] * un_
            ty = ty + thick[k] * vn_
        txs[pl.ds(own, BY), :] = tx
        typad[pl.ds(at, BY), :] = ty
        return carry

    lax.fori_loop(1, blocks - 1, speed_body, 0, unroll=3)
    wait_recv()
    for side, row in ((0, PAD - 1), (1, PAD + rows)):
        for f in range(3):
            for k in range(tiers):
                fields[f][k, pl.ds(row, 1), :] = ins_r[side, pl.ds(f * tiers + k, 1), :]
        levpad[pl.ds(row, 1), :] = ins_r[side, pl.ds(3 * tiers, 1), :]

    def combine(from_west, from_east):
        return jnp.where(odd, pltpu.roll(from_west, 1, 1), pltpu.roll(from_east, cols - 1, 1))

    lax.fori_loop(0, 2, lambda i, carry: speed_body(i * (blocks - 1), carry), 0)

    lev_own = iew_s[3 * pairs]
    lev_halo = combine(iew_r[0, 3 * pairs], iew_r[1, 3 * pairs])
    iew_c[3 * pairs] = lev_halo
    face = jnp.minimum(lev_own, lev_halo)
    face = face + pltpu.roll(face, cols // 2, 1)
    outward = jnp.where(odd, -1.0, 1.0)
    load = tx_edge = ty_edge = zero
    for h in range(pairs):
        own_, halo_ = [], []
        for f in range(3):
            own_.append(iew_s[f * pairs + h])
            halo_.append(combine(iew_r[0, f * pairs + h], iew_r[1, f * pairs + h]))
        (t, u, v), (th, uh, vh) = own_, halo_
        weight = jnp.where(high_half, thick[2 * h + 1], thick[2 * h])
        wet = face > jnp.where(high_half, 2.0 * h + 1.0, 2.0 * h)
        part = (-0.5 * HEAT_DILATION) * weight * (th - t)
        other = pltpu.roll(part, cols // 2, 1)
        slope = load + part + jnp.where(high_half, other, 0.0)
        load = load + part + other
        cu = TIME_STEP * jnp.where(wet, VISCOSITY * (uh - u) - outward * slope, 0.0)
        cv = TIME_STEP * jnp.where(wet, VISCOSITY * (vh - v), 0.0)
        ct = TIME_STEP * jnp.where(
            wet, DIFFUSIVITY * (th - t) - outward * (0.25 * (u + uh) * (t + th)), 0.0
        )
        iew_c[h] = ct
        iew_c[pairs + h] = cu
        iew_c[2 * pairs + h] = cv
        tx_edge = tx_edge + weight * cu
        ty_edge = ty_edge + weight * cv
    tx_edge = tx_edge + pltpu.roll(tx_edge, cols // 2, 1)
    ty_edge = ty_edge + pltpu.roll(ty_edge, cols // 2, 1)
    for j in range(blocks):
        here, shift = pl.ds(BY * j, BY), cols - 1 - 2 * j
        pad = pl.ds(PAD + BY * j, BY)
        txs[here, :] = txs[here, :] + jnp.where(edge, pltpu.roll(tx_edge, shift, 1), 0.0)
        typad[pad, :] = typad[pad, :] + jnp.where(edge, pltpu.roll(ty_edge, shift, 1), 0.0)

    def beside(value, halo):
        e = jnp.where(last, halo, pltpu.roll(value, cols - 1, 1))
        w = jnp.where(first, halo, pltpu.roll(value, 1, 1))
        return e, w

    def coefficients():
        for j in range(blocks):
            at, here = PAD + BY * j, pl.ds(BY * j, BY)
            lev = levpad[pl.ds(at, BY), :]
            lev_e, lev_w = beside(lev, pltpu.roll(iew_c[3 * pairs], cols - 1 - 2 * j, 1))
            lev_n = levpad[pl.ds(at + 1, BY), :]
            lev_s = levpad[pl.ds(at - 1, BY), :]
            h = depth(lev)
            surface = lev > 0
            link = [
                jnp.where(surface & (o > 0), 0.5 * (h + depth(o)), 0.0)
                for o in (lev_e, lev_w, lev_n, lev_s)
            ]
            diagonal = SURFACE_TERM + link[0] + link[1] + link[2] + link[3]
            sw[here, :] = jnp.where(surface, 1.0 / jnp.sqrt(diagonal), 0.0)
            dw[here, :] = jnp.where(surface, diagonal, 0.0)
            for ref, value in zip((le, lw, ln, ls), link):
                ref[here, :] = value

    def tracer_body(j, carry):
        at = pl.multiple_of(PAD + BY * j, BY)
        own = pl.multiple_of(BY * j, BY)
        lev, me, mn, ms = inner_faces(at)
        for k in range(tiers):
            t = tpad[k, pl.ds(at, BY), :]
            u = upad[k, pl.ds(at, BY), :]
            v = vpad[k, pl.ds(at, BY), :]
            te, ue = east_of(t), east_of(u)
            tn, ts = tpad[k, pl.ds(at + 1, BY), :], tpad[k, pl.ds(at - 1, BY), :]
            vn, vs = vpad[k, pl.ds(at + 1, BY), :], vpad[k, pl.ds(at - 1, BY), :]
            ge = jnp.where(me > k, DIFFUSIVITY * (te - t) - 0.25 * (u + ue) * (t + te), 0.0)
            flow = (
                (ge - west_of(ge))
                + jnp.where(mn > k, DIFFUSIVITY * (tn - t) - 0.25 * (v + vn) * (t + tn), 0.0)
                + jnp.where(ms > k, DIFFUSIVITY * (ts - t) + 0.25 * (v + vs) * (t + ts), 0.0)
            )
            shift = cols // 2 - 1 - 2 * j + (0 if k % 2 else cols // 2)
            ct, cu, cv = [
                jnp.where(edge, pltpu.roll(iew_c[f * pairs + k // 2], shift, 1), 0.0)
                for f in range(3)
            ]
            here = pl.ds(own, BY)
            tnext[k, here, :] = jnp.where(lev > k, t + TIME_STEP * flow, 0.0) + ct
            unext[k, here, :] = unext[k, here, :] + cu
            vnext[k, here, :] = vnext[k, here, :] + cv
        return carry

    def tracer_part(part, parts):
        lax.fori_loop(part * blocks // parts, (part + 1) * blocks // parts, tracer_body, 0)

    def block(j):
        return pl.ds(BY * j, BY)

    def send_surface(phase, ew_ref, ns_ref):
        acc = zero
        for j in range(blocks):
            acc = jnp.where(lax.div(lane, 2) == j, pltpu.roll(ew_ref(j), 2 * j + 1, 1), acc)
        sew_s[phase] = acc
        sns_s[phase, 0] = ns_ref[pl.ds(PAD + rows - 1, 1), :]
        sns_s[phase, 1] = ns_ref[pl.ds(PAD, 1), :]
        start, wait_recv, wait_send = exchange(
            sew_s.at[phase], sew_r.at[phase], sns_s.at[phase], sns_r.at[phase],
            sh_send.at[phase], sh_recv.at[phase],
        )
        start()
        finish.append(wait_send)
        return wait_recv

    def halo_of(phase, ns_ref):
        ns_ref[pl.ds(PAD - 1, 1), :] = sns_r[phase, 0]
        ns_ref[pl.ds(PAD + rows, 1), :] = sns_r[phase, 1]
        comb = combine(sew_r[phase, 0], sew_r[phase, 1])
        return lambda j: pltpu.roll(comb, cols - 1 - 2 * j, 1)

    def pad_block(j, move=0):
        return pl.ds(PAD + BY * j + move, BY)

    def operate(phase, ref, out):
        halo = halo_of(phase, ref)
        for j in range(blocks):
            x = ref[pad_block(j), :]
            e, w = beside(x, halo(j))
            out[block(j), :] = dw[block(j), :] * x - (
                le[block(j), :] * e
                + lw[block(j), :] * w
                + ln[block(j), :] * ref[pad_block(j, 1), :]
                + ls[block(j), :] * ref[pad_block(j, -1), :]
            )

    down = [jnp.where(sub >= d, ROW_DECAY**d, 0.0) for d in (1, 2, 4)]
    up = [jnp.where(sub < BY - d, ROW_DECAY**d, 0.0) for d in (1, 2, 4)]

    def condition(src, dst, scale=1.0, minus=()):
        scaled = sw[...] * src[...]
        high = scaled.astype(jnp.bfloat16)
        low = (scaled - high.astype(jnp.float32)).astype(jnp.bfloat16)
        both = jnp.dot(
            jnp.concatenate([high, low], axis=1), op_ref[...], preferred_element_type=jnp.float32
        )
        across = both[:, :cols] + both[:, cols:]
        for j in range(blocks):
            x = across[BY * j : BY * (j + 1), :]
            f = b = x
            for i, d in enumerate((1, 2, 4)):
                f = f + down[i] * pltpu.roll(f, d, 0)
                b = b + up[i] * pltpu.roll(b, BY - d, 0)
            y = scale * sw[block(j), :] * (f + b - x)
            for factor, ref in minus:
                y = y - factor * ref[pad_block(j), :]
            dst[pad_block(j), :] = y

    wait = send_surface(0, lambda j: txs[block(j), :], typad)
    coefficients()
    wait()
    halo = halo_of(0, typad)
    for j in range(blocks):
        e, w = beside(txs[block(j), :], halo(j))
        r = -0.5 * ((e - w) + (typad[pad_block(j, 1), :] - typad[pad_block(j, -1), :]))
        rr[block(j), :] = jnp.where(levpad[pad_block(j), :] > 0, r, 0.0)
    def dot(a, b):
        acc = zero
        for j in range(blocks):
            acc = acc + a(j) * b(j)
        return acc

    def at_block(ref):
        return lambda j: ref[block(j), :]

    def at_pad(ref):
        return lambda j: ref[pad_block(j), :]

    sums = {}
    for k in range(ITERS):
        if k == 0:
            condition(rr, basis[0])
        elif k == 1:
            condition(images[0], basis[1], 1.0 / RADIUS, ((CENTRE / RADIUS, basis[0]),))
        else:
            condition(
                images[k - 1], basis[k], 2.0 / RADIUS,
                ((2.0 * CENTRE / RADIUS, basis[k - 1]), (1.0, basis[k - 2])),
            )
        wait = send_surface(k + 1, at_pad(basis[k]), basis[k])
        sums["f", k] = dot(at_block(rr), at_pad(basis[k]))
        for i in range(k):
            sums[i, k] = dot(at_block(images[i]), at_pad(basis[k]))
        if k:
            sums[k - 1, k - 1] = dot(at_block(images[k - 1]), at_pad(basis[k - 1]))
        tracer_part(k, ITERS)
        if k + 1 == ITERS:
            keys = list(sums)
            tiles = [sums[key] for key in keys]
            tiles += [zero] * (SLOTS - len(tiles))
            width = 1
            while len(tiles) > 1:
                upper = lax.rem(lax.div(lane, width), 2) == 1
                half = len(tiles) // 2
                tiles = [
                    jnp.where(
                        upper,
                        tiles[i + half] + pltpu.roll(tiles[i + half], width, 1),
                        tiles[i] + pltpu.roll(tiles[i], cols - width, 1),
                    )
                    for i in range(half)
                ]
                width *= 2
            early = tiles[0]
        wait()
        operate(k + 1, basis[k], images[k])
    late = dot(at_block(images[-1]), at_pad(basis[-1]))
    width = 1
    while width < SLOTS:
        late = late + pltpu.roll(late, width, 1)
        width *= 2
    keys.append((ITERS - 1, ITERS - 1))

    def slot_of(i):
        at, bits = 0, SLOTS // 2
        width = 1
        while bits:
            at += width if i & bits else 0
            width *= 2
            bits //= 2
        return at

    final = slot_of(len(keys) - 1)
    both = jnp.where(lax.rem(lane, SLOTS) == final, late, early)
    ar_s[...] = jnp.sum(both, axis=0, keepdims=True)
    copies = [
        remote(ar_s, ar_r.at[i], ar_send.at[0], ar_recv.at[0], peer) for i, peer in enumerate(peers)
    ]
    for copy in copies:
        copy.start()
    pltpu.make_async_copy(ar_r, ar_r, ar_recv.at[0]).wait()
    total = ar_s[...]
    for i in range(len(peers)):
        total = total + ar_r[i]
    total = jnp.broadcast_to(total, (BY, cols))
    width = SLOTS
    while width < cols:
        total = total + pltpu.roll(total, width, 1)
        width *= 2
    value = {}
    for i, key in enumerate(keys):
        at = slot_of(i)
        value[key] = jnp.broadcast_to(total[:, at : at + 1], (BY, cols))
    gram = {(i, j): value[i, j] for j in range(ITERS) for i in range(j + 1)}
    rhs = [value["f", k] for k in range(ITERS)]
    floor = [1e-6 * gram[i, i] for i in range(ITERS)]
    inverse = []
    for i in range(ITERS):
        pivot = gram[i, i]
        usable = pivot > floor[i]
        inverse.append(jnp.where(usable, 1.0 / jnp.where(usable, pivot, 1.0), 0.0))
        for j in range(i + 1, ITERS):
            factor = gram[i, j] * inverse[i]
            rhs[j] = rhs[j] - factor * rhs[i]
            for k in range(j, ITERS):
                gram[j, k] = gram[j, k] - factor * gram[i, k]
    weights = [None] * ITERS
    for i in reversed(range(ITERS)):
        acc = rhs[i]
        for j in range(i + 1, ITERS):
            acc = acc - gram[i, j] * weights[j]
        weights[i] = acc * inverse[i]
    for j in range(blocks):
        x = weights[0] * basis[0][pad_block(j), :]
        for k in range(1, ITERS):
            x = x + weights[k] * basis[k][pad_block(j), :]
        height_ref[block(j), :] = x

    for wait_send in finish:
        wait_send()
    pltpu.make_async_copy(ar_r, ar_r, ar_send.at[0]).wait()


def write_kernel(*refs):
    sources, targets, sem = refs[:4], refs[4:8], refs[8]
    copies = [
        pltpu.make_async_copy(source, target, sem.at[i])
        for i, (source, target) in enumerate(zip(sources, targets))
    ]
    for copy in copies:
        copy.start()
    for copy in copies:
        copy.wait()


def local(heat_anomaly, zonal_speed, meridional_speed, submerged_tiers_per_site):
    tiers, rows, cols = heat_anomaly.shape
    nx, ny = lax.axis_size("lon"), lax.axis_size("lat")
    operator = jnp.asarray(column_operator(cols))
    f32 = jnp.float32
    field = jax.ShapeDtypeStruct((tiers, rows, cols), f32)
    shapes = (field, field, field, jax.ShapeDtypeStruct((rows, cols), f32))
    flat = pltpu.VMEM((rows, cols), f32)
    wide = pltpu.VMEM((rows + 2 * PAD, cols), f32)
    wide3 = pltpu.VMEM((tiers, rows + 2 * PAD, cols), f32)
    packs = 3 * (tiers // 2) + 1
    lines = 3 * tiers + BY
    phases = ITERS + 1
    others = nx * ny - 1
    any_spec = pl.BlockSpec(memory_space=pl.ANY)
    vmem_spec = pl.BlockSpec(memory_space=pltpu.VMEM)
    dma = pltpu.SemaphoreType.DMA
    results = pl.pallas_call(
        functools.partial(kernel, nx, ny, tiers, rows, cols),
        out_shape=shapes,
        in_specs=[any_spec] * 4 + [vmem_spec],
        out_specs=(vmem_spec,) * 4,
        scratch_shapes=[
            wide3, wide3, wide3, pltpu.VMEM((rows, cols), jnp.int32), wide,
            flat, wide, flat, flat, flat, flat, flat, flat,
            flat, wide, wide, wide, wide, flat, flat, flat, flat,
            pltpu.VMEM((2, lines, cols), f32),
            pltpu.VMEM((2, lines, cols), f32),
            pltpu.VMEM((packs, BY, cols), f32),
            pltpu.VMEM((2, packs, BY, cols), f32),
            pltpu.VMEM((packs, BY, cols), f32),
            pltpu.VMEM((phases, BY, cols), f32),
            pltpu.VMEM((phases, 2, BY, cols), f32),
            pltpu.VMEM((phases, 2, 1, cols), f32),
            pltpu.VMEM((phases, 2, 1, cols), f32),
            pltpu.VMEM((1, cols), f32),
            pltpu.VMEM((others, 1, cols), f32),
            dma((4,)), dma((4,)), dma((4,)),
            dma((phases, 4)), dma((phases, 4)), dma((1,)), dma((1,)),
        ],
        compiler_params=pltpu.CompilerParams(
            collective_id=0, has_side_effects=True, vmem_limit_bytes=60 * 1024 * 1024
        ),
        name="ocean_step",
    )(heat_anomaly, zonal_speed, meridional_speed, submerged_tiers_per_site, operator)
    return pl.pallas_call(
        write_kernel,
        out_shape=shapes,
        in_specs=[vmem_spec] * 4,
        out_specs=(any_spec,) * 4,
        scratch_shapes=[dma((4,))],
        name="write_results",
    )(*results)


def solution(mesh):
    placed = (
        P("groups", "lat", "lon"),
        P("groups", "lat", "lon"),
        P("groups", "lat", "lon"),
        P(("groups", "lat"), "lon"),
    )
    return jax.shard_map(
        local,
        mesh=mesh,
        in_specs=placed,
        out_specs=placed,
        check_vma=False,
    )
```
